256 devices in a mesh: blk: 16 (over x_hi, z), grp: 16 (over x_lo, y, core).
Axes of the slice: x: 4 (x_hi: 2, x_lo: 2; x = x_hi * 2 + x_lo), y: 4, z: 8, core: 2. Of those that a mesh axis runs over, the one named last changes fastest.
Arguments:
- queries: bfloat16 [16, 2048, 4096], P('grp', 'blk'), may hold values from -72 to 72
- question_pos: int32 [16, 2048], P('grp', 'blk'), may hold values from 0 to 1023
- cache_limit: int32 [16, 2048], P('grp', 'blk'), may hold values from 256 to 1024
- cache: bfloat16 [1024, 2048], P('blk'), may hold values from -6 to 6
- prefix: bfloat16 [2, 8, 128, 128], replicated, may hold values from -6 to 6
Outputs:
- prefix_step: float32 [2048, 128], P(('blk', 'grp'))
- row_error: float32 [16, 2048], P('grp', 'blk')
The draws below stay inside these ranges and needn't reach their ends.
All inputs are finite; a program needn't handle non-finite values.
Results may differ from the reference program's by a relative error of at most 0.012.
The reference program's roundings to bfloat16 on the way count: a program that leaves them out, or rounds other values in their place, can miss the bound.
Values may be sent and summed in bfloat16 or wider, within the bound.
A program may use at most 64 MiB of HBM per device.

```python
import jax
import jax.numpy as jnp
from jax import lax

QH = 32
KVH = 8
HD = 128
QROWS = 128
P_SIZE = 128
QLEN = 1024
GROUPS = 16
GQROWS = 2048
CACHE = 1024


def draw_queries(key, part):
    normal_key = jax.random.fold_in(jax.random.fold_in(key, 11), 0)
    extent = (GROUPS, GQROWS, QH * HD)
    return jnp.clip(jax.random.normal(normal_key, extent, jnp.float32), -6.0, 6.0).astype(jnp.bfloat16)


def plant(entries, key, least, high):
    longest = entries.shape.index(max(entries.shape))
    spots = []
    for shift in (0, 1):
        where = [jax.random.randint(jax.random.fold_in(key, axis), (), 0, length) for axis, length in enumerate(entries.shape)]
        where[longest] = (where[longest] + shift) % entries.shape[longest]
        spots.append(tuple(where))
    return entries.at[spots[0]].set(least).at[spots[1]].set(high)


def block_levels(stream_key, dims, cuts, smallest, largest):
    def one(dim, parts):
        heights = jax.random.uniform(jax.random.fold_in(jax.random.fold_in(stream_key, 6), dim), (parts,), jnp.float32, smallest / len(cuts), largest / len(cuts))
        return jnp.repeat(jnp.exp(heights), dims[dim] // parts).reshape((-1,) + (1,) * (len(dims) - dim - 1))

    level = one(*cuts[0])
    for cut in cuts[1:]:
        level = level * one(*cut)
    return level


def normal_values(stream_key, shape, scale, bound, cuts=(), held_as=jnp.bfloat16):
    entries = jax.random.normal(stream_key, shape, jnp.float32) * scale
    if len(cuts) > 0:
        entries = block_levels(stream_key, shape, cuts, -0.22, 0.18) * entries
    return jnp.clip(entries, min=-bound, max=bound).astype(held_as)


def setup_inputs(seed: int = 0) -> dict:
    key_list = jax.random.split(jax.random.key(seed), 6)
    return {
        "queries": draw_queries(jax.random.fold_in(key_list[5], 71), 0),
        "question_pos": plant(jax.random.randint(key_list[1], (GROUPS, GQROWS), 0, QLEN), jax.random.fold_in(key_list[1], 1), 0, QLEN - 1).astype(jnp.int32),
        "cache_limit": plant(jax.random.randint(key_list[2], (GROUPS, GQROWS), CACHE // 4, CACHE + 1), jax.random.fold_in(key_list[2], 1), CACHE // 4, CACHE).astype(jnp.int32),
        "cache": normal_values(key_list[3], (CACHE, 2 * KVH * HD), 1.0, 6.0, ((0, 16),)),
        "prefix": normal_values(key_list[4], (2, KVH, P_SIZE, HD), 1.0, 6.0),
    }


rope_base = 500000.0
neg_fill = -1e+30
norm_eps = 1e-06

def rotate(vectors, positions):
    halfway = vectors.shape[-1] // 2
    frequency = rope_base ** (-jnp.arange(halfway, dtype=jnp.float32) / halfway)
    angles = positions.astype(jnp.float32)[:, None] * frequency[None, :]
    cosine = jnp.cos(angles)[:, None, :]
    sine_part = jnp.sin(angles)[:, None, :]
    values = vectors.astype(jnp.float32)
    leading = values[..., :halfway]
    trailing = values[..., halfway:]
    turned = jnp.concatenate([leading * cosine - trailing * sine_part, trailing * cosine + leading * sine_part], axis=-1)
    return turned.astype(jnp.bfloat16)

def teacher_block(teacher_q, limits, cache):
    row_count = teacher_q.shape[0]
    key_width = KVH * HD
    key_part = cache[:, :key_width].reshape(CACHE, KVH, HD).astype(jnp.float32)
    value_part = cache[:, key_width:].reshape(CACHE, KVH, HD).astype(jnp.float32)
    grouped = teacher_q.reshape(row_count, KVH, QH // KVH, HD).astype(jnp.float32)
    scores = jnp.einsum('rcgd,jcd->rcgj', grouped, key_part, precision=lax.Precision.HIGHEST) * HD ** (-0.5)
    visible = (jnp.arange(CACHE, dtype=jnp.int32)[None, :] < limits[:, None])[:, None, None, :]
    masked = jnp.where(visible, scores, neg_fill)
    highest = lax.optimization_barrier(jnp.max(masked, axis=-1, keepdims=True))
    raised = jnp.where(visible, jnp.exp(masked - highest), 0.0)
    totals = lax.optimization_barrier(jnp.sum(raised, axis=-1))
    rounded = lax.optimization_barrier(raised.astype(jnp.bfloat16)).astype(jnp.float32)
    mixture = jnp.einsum('rcgj,jcd->rcgd', rounded, value_part, precision=lax.Precision.HIGHEST)
    return mixture / totals[..., None]

def student_block(student_q, prefix, target):
    row_count = student_q.shape[0]
    grouped = student_q.reshape(row_count, KVH, QH // KVH, HD).astype(jnp.float32)
    key_part = prefix[0].astype(jnp.float32)
    value_part = prefix[1].astype(jnp.float32)
    scaling = HD ** (-0.5)
    scores = jnp.einsum('rcgd,cpd->rcgp', grouped, key_part, precision=lax.Precision.HIGHEST) * scaling
    raised = jnp.exp(scores - lax.optimization_barrier(jnp.max(scores, axis=-1, keepdims=True)))
    weights = raised / lax.optimization_barrier(jnp.sum(raised, axis=-1, keepdims=True))
    rounded = lax.optimization_barrier(weights.astype(jnp.bfloat16)).astype(jnp.float32)
    output = jnp.einsum('rcgp,cpd->rcgd', rounded, value_part, precision=lax.Precision.HIGHEST)
    difference = output - target
    cotangent = lax.optimization_barrier(difference.astype(jnp.bfloat16)).astype(jnp.float32)
    grad_values = jnp.einsum('rcgp,rcgd->cpd', rounded, cotangent, precision=lax.Precision.HIGHEST)
    along_values = jnp.einsum('rcgd,cpd->rcgp', cotangent, value_part, precision=lax.Precision.HIGHEST)
    inner_sum = lax.optimization_barrier(jnp.sum(weights * along_values, axis=-1, keepdims=True))
    score_grad = lax.optimization_barrier((weights * (along_values - inner_sum) * scaling).astype(jnp.bfloat16)).astype(jnp.float32)
    grad_keys = jnp.einsum('rcgp,rcgd->cpd', score_grad, grouped, precision=lax.Precision.HIGHEST)
    row_error = jnp.sqrt(lax.optimization_barrier(jnp.mean(difference * difference, axis=(1, 2, 3)))) / jnp.sqrt(lax.optimization_barrier(jnp.mean(target * target, axis=(1, 2, 3))) + norm_eps)
    return (row_error, jnp.stack([grad_keys, grad_values]))

def reference(queries, question_pos, cache_limit, cache, prefix):
    blocks = queries.reshape(-1, QROWS, QH, HD)
    positions = question_pos.reshape(-1, QROWS)
    limits = cache_limit.reshape(-1, QROWS)

    def visit_block(summed, element):
        block_q, block_pos, block_lim = element
        teacher_q = rotate(block_q, block_lim + block_pos)
        student_q = rotate(block_q, P_SIZE + block_pos)
        target = teacher_block(teacher_q, block_lim, cache)
        row_error, gradient = student_block(student_q, prefix, target)
        return (summed + gradient, row_error)
    start_sum = jnp.zeros((2, KVH, P_SIZE, HD), jnp.float32)
    gradient, errors = lax.scan(visit_block, start_sum, (blocks, positions, limits))
    flattened = gradient.reshape(2 * KVH * P_SIZE, HD)
    prefix_step = flattened / jnp.sqrt(jnp.mean(flattened * flattened) + norm_eps)
    return (prefix_step, errors.reshape(GROUPS, GQROWS))
```

```python
import math

import jax
import jax.numpy as jnp
import numpy as np
from jax import lax
from jax.experimental import pallas as pl
from jax.experimental.pallas import tpu as pltpu
from jax.sharding import PartitionSpec as P

MESH = pl.DeviceIdType.MESH
rope_base = 500000.0
neg_fill = -1e30
norm_eps = 1e-06

HD = 128
KVH = 8
PER = 4
ROWS = 128
POS = 1024
SHARD = 64
PRE = 128
FEATURES = KVH * PER * HD
WIDE = PER * HD
KEYS = KVH * HD
SCALE = HD**-0.5
SCALE_LOG2E = SCALE * math.log2(math.e)

ORDER = (0, 1, 2, 3, 6, 7, 4, 5)


def coords():
    b, g = lax.axis_index("blk"), lax.axis_index("grp")
    return (b // 8) * 2 + g // 8, (g // 2) % 4, b % 8, g % 2


def device(x, y, z, c):
    return ((x // 2) * 8 + z, (x % 2) * 8 + y * 2 + c)


def sincos(angle):
    k = jnp.floor(angle * (2.0 / math.pi) + 0.5)
    r = angle - k * 1.5703125
    r = r - k * 4.837512969970703125e-4
    r = r - k * 7.54978995489188216e-8
    r2 = r * r
    s = r + r * r2 * (-1.6666654611e-1 + r2 * (8.3321608736e-3 + r2 * -1.9515295891e-4))
    c = 1.0 + r2 * (
        -0.5 + r2 * (4.166664568298827e-2 + r2 * (-1.388731625493765e-3 + r2 * 2.443315711809948e-5))
    )
    n = k.astype(jnp.int32)
    odd = (n & 1) == 1
    sine = jnp.where(odd, c, s)
    cosine = jnp.where(odd, s, c)
    sine = jnp.where((n & 2) == 2, -sine, sine)
    cosine = jnp.where(((n + 1) & 2) == 2, -cosine, cosine)
    return sine, cosine


def dot(a, b, ca, cb):
    return lax.dot_general(a, b, (((ca,), (cb,)), ((), ())), preferred_element_type=jnp.float32)


def rows_as_sublanes(row):
    return jnp.broadcast_to(row, (ROWS, ROWS)).T


def block_math(q, pos_row, lim_row, freq, keys, values, pk, pv):
    pos = rows_as_sublanes(pos_row.astype(jnp.float32))
    lim_f = rows_as_sublanes(lim_row.astype(jnp.float32))
    lane = lax.broadcasted_iota(jnp.int32, (ROWS, HD), 1)
    low = lane < HD // 2
    st, ct = sincos((lim_f + pos) * freq)
    ss, cs = sincos((PRE + pos) * freq)
    st = jnp.where(low, -st, st)
    ss = jnp.where(low, -ss, ss)
    lim = lim_f.astype(jnp.int32)
    student_q = []
    targets = []
    for h in range(PER):
        v = q[:, h * HD : (h + 1) * HD].astype(jnp.float32)
        vr = pltpu.roll(v, HD // 2, 1)
        student_q.append((v * cs + vr * ss).astype(jnp.bfloat16))
        tq = (v * ct + vr * st).astype(jnp.bfloat16)
        scores = dot(tq, keys, 1, 1)
        parts = []
        for j in range(POS // HD):
            part = scores[:, j * HD : (j + 1) * HD]
            if j >= 2:
                part = jnp.where(lane + j * HD < lim, part, neg_fill)
            parts.append(part)
        top = parts[0]
        for part in parts[1:]:
            top = jnp.maximum(top, part)
        top = jnp.max(top, axis=1, keepdims=True)
        total = None
        weights = []
        for part in parts:
            e = jnp.exp2((part - top) * SCALE_LOG2E)
            total = e if total is None else total + e
            weights.append(e.astype(jnp.bfloat16))
        total = jnp.sum(total, axis=1, keepdims=True)
        mixture = dot(jnp.concatenate(weights, axis=1), values, 1, 0)
        targets.append(mixture * (1.0 / total))
    sq = jnp.concatenate(student_q, axis=0)
    target = jnp.concatenate(targets, axis=0)
    scores = dot(sq, pk, 1, 1)
    raised = jnp.exp2((scores - jnp.max(scores, axis=1, keepdims=True)) * SCALE_LOG2E)
    probs = raised * (1.0 / jnp.sum(raised, axis=1, keepdims=True))
    rounded = probs.astype(jnp.bfloat16)
    out = dot(rounded, pv, 1, 0)
    diff = out - target
    cot = diff.astype(jnp.bfloat16)
    along = dot(cot, pv, 1, 1)
    inner = jnp.sum(probs * along, axis=1, keepdims=True)
    grad = (probs * (along - inner) * SCALE).astype(jnp.bfloat16)
    gv = dot(rounded, cot, 0, 0)
    gk = dot(grad, sq, 0, 0)
    d2 = diff * diff
    t2 = target * target
    dsum = d2[0:ROWS] + d2[ROWS : 2 * ROWS] + d2[2 * ROWS : 3 * ROWS] + d2[3 * ROWS :]
    tsum = t2[0:ROWS] + t2[ROWS : 2 * ROWS] + t2[2 * ROWS : 3 * ROWS] + t2[3 * ROWS :]
    derr = jnp.sum(dsum.T, axis=0, keepdims=True)
    terr = jnp.sum(tsum.T, axis=0, keepdims=True)
    return gk, gv, derr, terr


def kernel(
    q_hbm, pos_ref, lim_ref, cache_hbm, prefix_hbm, freq_ref,
    step_ref, err_ref,
    qbuf, ibuf, istage, kv, pbuf, grad, xland, xsum, zland, own8, eland, eout, nsend, nland, fin,
    local_sem, qs, qr, is_, ir, zs, zr, fs, fr, es, er, gxs, gxr, gzs, gzr, ps, pr, ns, nr,
):
    x, y, z, c = coords()
    x_hi, x_lo = x // 2, x % 2
    head = y * 2 + c

    def yc(k):
        return (y + k // 2) % 4, (c + k) % 2

    def yc_dev(k):
        yy, cc = yc(k)
        return device(x, yy, z, cc)

    def z_dev(k):
        return device(x, y, (z + k) % 8, c)

    def x_dev(k):
        return device((x + k) % 4, y, z, c)

    own_perm = z == head
    perm_dev = device(x, z // 2, head, z % 2)

    def remote(src, dst, ssem, rsem, dev):
        return pltpu.make_async_remote_copy(
            src_ref=src, dst_ref=dst, send_sem=ssem, recv_sem=rsem,
            device_id=dev, device_id_type=MESH,
        )

    def cols(start, n):
        return pl.ds(pl.multiple_of(start, HD), n)

    barrier = pltpu.get_barrier_semaphore()
    for k in range(1, 8):
        pl.semaphore_signal(barrier, inc=1, device_id=yc_dev(k), device_id_type=MESH)
        pl.semaphore_signal(barrier, inc=1, device_id=z_dev(k), device_id_type=MESH)
    for k in range(1, 4):
        pl.semaphore_signal(barrier, inc=1, device_id=x_dev(k), device_id_type=MESH)

    @pl.when(jnp.logical_not(own_perm))
    def _():
        pl.semaphore_signal(barrier, inc=1, device_id=perm_dev, device_id_type=MESH)

    own_rows = pl.ds(pl.multiple_of((x_hi * 8 + z) * SHARD, SHARD), SHARD)
    lc = [
        pltpu.make_async_copy(q_hbm.at[0, :, cols(head * WIDE, WIDE)], qbuf.at[head], local_sem.at[0]),
        pltpu.make_async_copy(
            cache_hbm.at[:, cols(x_lo * KEYS + head * HD, HD)], kv.at[x_lo, own_rows], local_sem.at[1]
        ),
        pltpu.make_async_copy(prefix_hbm.at[:, head], pbuf, local_sem.at[2]),
    ]
    for cp in lc:
        cp.start()
    istage[0:1, :] = pos_ref[...]
    istage[1:2, :] = lim_ref[...]
    ibuf[head, 0:1, :] = pos_ref[...]
    ibuf[head, 1:2, :] = lim_ref[...]

    pl.semaphore_wait(barrier, jnp.where(own_perm, 17, 18))

    lc[1].wait()
    zc = []
    for k in (1, 7, 2, 6, 3, 5, 4):
        cp = remote(kv.at[x_lo, own_rows], kv.at[x_lo, own_rows], zs.at[k], zr.at[k], z_dev(k))
        cp.start()
        zc.append(cp)
    qc = []
    for k in (1, 2, 3, 6, 7, 4, 5):
        yy, cc = yc(k)
        cp = remote(istage, ibuf.at[head], is_.at[k], ir.at[k], yc_dev(k))
        cp.start()
        qc.append(cp)
        cp = remote(
            q_hbm.at[0, :, cols((yy * 2 + cc) * WIDE, WIDE)], qbuf.at[head], qs.at[k], qr.at[k], yc_dev(k)
        )
        cp.start()
        qc.append(cp)
    for cp in zc:
        cp.wait()
    half = pl.ds(pl.multiple_of(x_hi * 512, 512), 512)
    fc = []
    for k in (1, 3, 2):
        cp = remote(kv.at[x_lo, half], kv.at[x_lo, half], fs.at[k], fr.at[k], x_dev(k))
        cp.start()
        fc.append(cp)
    lc[0].wait()
    lc[2].wait()
    for cp in fc:
        cp.wait()
    for cp in qc:
        cp.wait()

    freq = freq_ref[0:1, :]
    pk = pbuf[0]
    pv = pbuf[1]
    grad[...] = jnp.zeros_like(grad)

    def work(slot):
        gk, gv, derr, terr = block_math(
            qbuf[slot], ibuf[slot, 0:1, :], ibuf[slot, 1:2, :], freq, kv[0], kv[1], pk, pv
        )
        grad[0] += gk
        grad[1] += gv
        eout[slot, 0:1, :] = derr
        eout[slot, 1:2, :] = terr

    def body(i, carry):
        k = i
        work(((y + k // 2) % 4) * 2 + (c + k) % 2)
        return carry

    lax.fori_loop(0, 8, body, 0)

    gx = []
    for k in (1, 3, 2):
        xx = (x + k) % 4
        cp = remote(
            grad.at[xx // 2, pl.ds(pl.multiple_of((xx % 2) * 64, 64), 64)], xland.at[k], gxs.at[k], gxr.at[k], x_dev(k)
        )
        cp.start()
        gx.append(cp)
    ec = []
    for k in range(1, 8):
        yy, cc = yc(k)
        cp = remote(eout.at[yy * 2 + cc], eland.at[head], es.at[k], er.at[k], yc_dev(k))
        cp.start()
        ec.append(cp)
    eland[head] = eout[head]
    for cp in gx:
        cp.wait()
    xsum[...] = (
        grad[x_hi, pl.ds(pl.multiple_of(x_lo * 64, 64), 64), :] + xland[1] + xland[2] + xland[3]
    )
    gz = []
    for k in (4, 3, 5, 2, 6, 1, 7):
        zz = (z + k) % 8
        cp = remote(
            xsum.at[pl.ds(pl.multiple_of(zz * 8, 8), 8)], zland.at[k], gzs.at[k], gzr.at[k], z_dev(k)
        )
        cp.start()
        gz.append(cp)
    zland[0] = xsum[pl.ds(pl.multiple_of(z * 8, 8), 8), :]
    for cp in gz:
        cp.wait()
    rows8 = zland[0]
    for k in range(1, 8):
        rows8 = rows8 + zland[k]
    own8[...] = rows8

    @pl.when(jnp.logical_not(own_perm))
    def _():
        cp = remote(own8, fin, ps.at[0], pr.at[0], perm_dev)
        cp.start()

    @pl.when(own_perm)
    def _():
        fin[...] = own8[...]

    nsend[0] = jnp.broadcast_to(jnp.sum(rows8 * rows8, axis=0, keepdims=True), (8, HD))

    def exchange(stage, ks, dev):
        cps = []
        for k in ks:
            cp = remote(nsend.at[stage], nland.at[stage, k], ns.at[stage, k], nr.at[stage, k], dev(k))
            cp.start()
            cps.append(cp)
        for cp in cps:
            cp.wait()
        acc = nsend[stage]
        for k in ks:
            acc = acc + nland[stage, k]
        return acc

    nsend[1] = exchange(0, range(1, 8), yc_dev)
    nsend[2] = exchange(1, range(1, 4), x_dev)
    for cp in ec:
        cp.wait()
    esum = eland[0]
    for k in range(1, 8):
        esum = esum + eland[k]
    err_ref[...] = jnp.sqrt(esum[0:1] / FEATURES) / jnp.sqrt(esum[1:2] / FEATURES + norm_eps)

    @pl.when(jnp.logical_not(own_perm))
    def _():
        remote(own8, fin, ps.at[0], pr.at[0], perm_dev).wait()

    whole = exchange(2, range(1, 8), z_dev)
    mean_square = jnp.sum(whole, axis=1, keepdims=True) / (2.0 * KVH * PRE * HD)
    step_ref[...] = fin[...] / jnp.sqrt(mean_square + norm_eps)


def frequencies():
    f = (rope_base ** (-np.arange(HD // 2, dtype=np.float64) / (HD // 2))).astype(np.float32)
    return np.broadcast_to(np.concatenate([f, f])[None, :], (8, HD)).copy()


def shards(queries, question_pos, cache_limit, cache, prefix):
    freq = jnp.asarray(frequencies())
    vmem = pl.BlockSpec(memory_space=pltpu.VMEM)
    hbm = pl.BlockSpec(memory_space=pltpu.HBM)
    f32, bf16 = jnp.float32, jnp.bfloat16
    dma = pltpu.SemaphoreType.DMA
    return pl.pallas_call(
        kernel,
        out_shape=(
            jax.ShapeDtypeStruct((8, HD), f32),
            jax.ShapeDtypeStruct((1, ROWS), f32),
        ),
        in_specs=[hbm, vmem, vmem, hbm, hbm, vmem],
        out_specs=(vmem, vmem),
        scratch_shapes=[
            pltpu.VMEM((8, ROWS, WIDE), bf16),
            pltpu.VMEM((8, 8, ROWS), jnp.int32),
            pltpu.VMEM((8, ROWS), jnp.int32),
            pltpu.VMEM((2, POS, HD), bf16),
            pltpu.VMEM((2, PRE, HD), bf16),
            pltpu.VMEM((2, PRE, HD), f32),
            pltpu.VMEM((4, 64, HD), f32),
            pltpu.VMEM((64, HD), f32),
            pltpu.VMEM((8, 8, HD), f32),
            pltpu.VMEM((8, HD), f32),
            pltpu.VMEM((8, 8, ROWS), f32),
            pltpu.VMEM((8, 8, ROWS), f32),
            pltpu.VMEM((3, 8, HD), f32),
            pltpu.VMEM((3, 8, 8, HD), f32),
            pltpu.VMEM((8, HD), f32),
            dma((3,)),
            dma((8,)), dma((8,)), dma((8,)), dma((8,)), dma((8,)), dma((8,)), dma((4,)), dma((4,)),
            dma((8,)), dma((8,)), dma((4,)), dma((4,)), dma((8,)), dma((8,)), dma((1,)), dma((1,)),
            dma((3, 8)), dma((3, 8)),
        ],
        compiler_params=pltpu.CompilerParams(
            collective_id=0, has_side_effects=True, vmem_limit_bytes=48 * 1024 * 1024
        ),
        cost_estimate=pl.CostEstimate(
            flops=3_000_000_000, bytes_accessed=4_000_000, transcendentals=5_000_000
        ),
    )(queries, question_pos, cache_limit, cache, prefix, freq)


def solution(mesh):
    return jax.shard_map(
        shards,
        mesh=mesh,
        in_specs=(P("grp", "blk", None), P("grp", "blk"), P("grp", "blk"), P("blk", None), P()),
        out_specs=(P(("blk", "grp"), None), P("grp", "blk")),
        check_vma=False,
    )
```

```python
import math

import jax
import jax.numpy as jnp
import numpy as np
from jax import lax
from jax.experimental import pallas as pl
from jax.experimental.pallas import tpu as pltpu
from jax.sharding import PartitionSpec as P

MESH = pl.DeviceIdType.MESH
rope_base = 500000.0
neg_fill = -1e30
norm_eps = 1e-06

HD = 128
KVH = 8
PER = 4
ROWS = 128
POS = 1024
SHARD = 64
PRE = 128
FEATURES = KVH * PER * HD
WIDE = PER * HD
KEYS = KVH * HD
SCALE = HD**-0.5
SCALE_LOG2E = SCALE * math.log2(math.e)


def coords():
    b, g = lax.axis_index("blk"), lax.axis_index("grp")
    return (b // 8) * 2 + g // 8, (g // 2) % 4, b % 8, g % 2


def device(x, y, z, c):
    return ((x // 2) * 8 + z, (x % 2) * 8 + y * 2 + c)


def sincos(angle):
    k = jnp.floor(angle * (2.0 / math.pi) + 0.5)
    r = angle - k * 1.5703125
    r = r - k * 4.837512969970703125e-4
    r = r - k * 7.54978995489188216e-8
    r2 = r * r
    s = r + r * r2 * (-1.6666654611e-1 + r2 * (8.3321608736e-3 + r2 * -1.9515295891e-4))
    c = 1.0 + r2 * (
        -0.5 + r2 * (4.166664568298827e-2 + r2 * (-1.388731625493765e-3 + r2 * 2.443315711809948e-5))
    )
    n = k.astype(jnp.int32)
    odd = (n & 1) == 1
    sine = jnp.where(odd, c, s)
    cosine = jnp.where(odd, s, c)
    sine = jnp.where((n & 2) == 2, -sine, sine)
    cosine = jnp.where(((n + 1) & 2) == 2, -cosine, cosine)
    return sine, cosine


def dot(a, b, ca, cb):
    return lax.dot_general(a, b, (((ca,), (cb,)), ((), ())), preferred_element_type=jnp.float32)


RC = 256
JC = 256

def teacher(q, pos_row, lim_row, freq_col, keys, values_t, eye):
    pos = pos_row.astype(jnp.float32)
    lim = lim_row.astype(jnp.float32)
    half = HD // 2
    st, ct = sincos(freq_col * (lim + pos))
    ss, cs = sincos(freq_col * (PRE + pos))
    qt = [dot(eye, q[:, h * HD : (h + 1) * HD], 1, 1) for h in range(PER)]
    def turned(cosine, sine):
        parts = []
        for h in range(PER):
            lead, trail = qt[h][:half], qt[h][half:]
            parts.append(
                jnp.concatenate(
                    [lead * cosine - trail * sine, trail * cosine + lead * sine], axis=0
                ).astype(jnp.bfloat16)
            )
        return parts
    tq = turned(ct, st)
    sq = turned(cs, ss)
    targets = []
    for r in range(0, PER, RC // HD):
        n = RC // HD
        part_q = jnp.concatenate(tq[r : r + n], axis=1)
        limits = jnp.concatenate([lim_row] * n, axis=1)
        parts = []
        top = None
        for j in range(0, POS, JC):
            part = dot(keys[j : j + JC], part_q, 1, 0)
            if j >= 256:
                where = lax.broadcasted_iota(jnp.int32, (JC, RC), 0) + j
                part = jnp.where(where < limits, part, neg_fill)
            parts.append(part)
            m = jnp.max(part, axis=0, keepdims=True)
            top = m if top is None else jnp.maximum(top, m)
        total = None
        mixture = None
        for a, part in enumerate(parts):
            e = jnp.exp2((part - top) * SCALE_LOG2E)
            t = jnp.sum(e, axis=0, keepdims=True)
            total = t if total is None else total + t
            o = dot(values_t[:, a * JC : (a + 1) * JC], e.astype(jnp.bfloat16), 1, 0)
            mixture = o if mixture is None else mixture + o
        targets.append(mixture * (1.0 / total))
    return jnp.concatenate(targets, axis=1), jnp.concatenate(sq, axis=1)

def student(sq, target, pk, pv, pv_t):
    scores = dot(pk, sq, 1, 0)
    raised = jnp.exp2((scores - jnp.max(scores, axis=0, keepdims=True)) * SCALE_LOG2E)
    probs = raised * (1.0 / jnp.sum(raised, axis=0, keepdims=True))
    rounded = probs.astype(jnp.bfloat16)
    out = dot(pv_t, rounded, 1, 0)
    diff = out - target
    cot = diff.astype(jnp.bfloat16)
    along = dot(pv, cot, 1, 0)
    inner = jnp.sum(probs * along, axis=0, keepdims=True)
    grad = (probs * (along - inner) * SCALE).astype(jnp.bfloat16)
    gv = dot(rounded, cot, 1, 1)
    gk = dot(grad, sq, 1, 1)
    d = jnp.sum(diff * diff, axis=0, keepdims=True)
    t = jnp.sum(target * target, axis=0, keepdims=True)
    return gk, gv, d, t

def heads_sum(d):
    return d[:, :ROWS] + d[:, ROWS : 2 * ROWS] + d[:, 2 * ROWS : 3 * ROWS] + d[:, 3 * ROWS :]


def far_first(k):
    dx, dz = k // 8, k % 8
    return -(min(dx, 4 - dx) + min(dz, 8 - dz))


PLANE = sorted(range(1, 32), key=far_first)


def kernel(
    q_hbm, pos_hbm, lim_hbm, cache_hbm, prefix_hbm, freq_hbm,
    step_ref, err_ref,
    qbuf, ibuf, istage, freq, kv, vt, pbuf, pvt, eye, grad, rland, own8, eland, eout, nsend, nyc, nxz, fin,
    local_sem, qs, qr, is_, ir, zs, zr, fs, fr, es, er, gs, gr, ps, pr, ns, nr,
):
    x, y, z, c = coords()
    x_hi, x_lo = x // 2, x % 2
    head = y * 2 + c

    def yc(k):
        return (y + k // 2) % 4, (c + k) % 2

    def yc_dev(k):
        yy, cc = yc(k)
        return device(x, yy, z, cc)

    def z_dev(k):
        return device(x, y, (z + k) % 8, c)

    def x_dev(k):
        return device((x + k) % 4, y, z, c)

    def xz(k):
        return (x + k // 8) % 4, (z + k % 8) % 8

    def xz_dev(k):
        xx, zz = xz(k)
        return device(xx, y, zz, c)

    own_perm = z == head
    perm_dev = device(x, z // 2, head, z % 2)

    def remote(src, dst, ssem, rsem, dev):
        return pltpu.make_async_remote_copy(
            src_ref=src, dst_ref=dst, send_sem=ssem, recv_sem=rsem,
            device_id=dev, device_id_type=MESH,
        )

    def cols(start, n):
        return pl.ds(pl.multiple_of(start, HD), n)

    def shard_rows(zz):
        return pl.ds(pl.multiple_of((x_hi * 8 + zz) * SHARD, SHARD), SHARD)

    barrier = pltpu.get_barrier_semaphore()
    for k in range(1, 8):
        pl.semaphore_signal(barrier, inc=1, device_id=z_dev(k), device_id_type=MESH)
        pl.semaphore_signal(barrier, inc=1, device_id=yc_dev(k), device_id_type=MESH)
    for k in range(1, 4):
        pl.semaphore_signal(barrier, inc=1, device_id=x_dev(k), device_id_type=MESH)

    own_rows = shard_rows(z)
    lc = [
        pltpu.make_async_copy(
            cache_hbm.at[:, cols(x_lo * KEYS + head * HD, HD)], kv.at[x_lo, own_rows], local_sem.at[0]
        ),
        pltpu.make_async_copy(pos_hbm, istage.at[pl.ds(0, 1)], local_sem.at[1]),
        pltpu.make_async_copy(lim_hbm, istage.at[pl.ds(1, 1)], local_sem.at[2]),
        pltpu.make_async_copy(q_hbm.at[0, :, cols(head * WIDE, WIDE)], qbuf.at[head], local_sem.at[3]),
        pltpu.make_async_copy(prefix_hbm.at[:, head], pbuf, local_sem.at[4]),
        pltpu.make_async_copy(freq_hbm, freq, local_sem.at[5]),
    ]
    for cp in lc:
        cp.start()
    grad[...] = jnp.zeros_like(grad)
    eye[...] = jnp.where(
        lax.broadcasted_iota(jnp.int32, (HD, HD), 0) == lax.broadcasted_iota(jnp.int32, (HD, HD), 1), 1.0, 0.0
    ).astype(jnp.bfloat16)
    lc[0].wait()
    lc[1].wait()
    lc[2].wait()

    pl.semaphore_wait(barrier, 17)

    sent = []
    zc = {}
    for k in (1, 7, 2, 6, 3, 5, 4):
        zc[k] = remote(kv.at[x_lo, own_rows], kv.at[x_lo, own_rows], zs.at[k], zr.at[k], z_dev(k))
        zc[k].start()
        sent.append(zc[k])
    fc = []

    def forward(k):
        rows = shard_rows((z + 8 - k) % 8)
        for n in (1, 3, 2):
            cp = remote(kv.at[x_lo, rows], kv.at[x_lo, rows], fs.at[k, n], fr.at[k, n], x_dev(n))
            cp.start()
            fc.append(cp)
            sent.append(cp)

    forward(0)
    for k in (1, 2, 3, 6, 7, 4, 5):
        yy, cc = yc(k)
        cp = remote(istage, ibuf.at[head], is_.at[k], ir.at[k], yc_dev(k))
        cp.start()
        sent.append(cp)
        cp = remote(
            q_hbm.at[0, :, cols((yy * 2 + cc) * WIDE, WIDE)], qbuf.at[head], qs.at[k], qr.at[k], yc_dev(k)
        )
        cp.start()
        sent.append(cp)
    for k in (1, 7, 2, 6, 3, 5, 4):
        zc[k].wait_recv()
        forward(k)
    ibuf[head] = istage[...]
    lc[3].wait()
    lc[4].wait()
    lc[5].wait()
    pvt[...] = pbuf[1].T
    for cp in fc:
        cp.wait_recv()
    vt[...] = kv[1].T

    def body(p, carry):
        dy = p ^ (p >> 1)
        kk = ((4 - dy) % 4) * 2
        base = ((y + dy) % 4) * 2
        a, b = base + c, base + 1 - c

        @pl.when(p > 0)
        def _():
            remote(istage, ibuf.at[a], is_.at[kk], ir.at[kk], yc_dev(2)).wait_recv()
            remote(qbuf.at[a], qbuf.at[a], qs.at[kk], qr.at[kk], yc_dev(2)).wait_recv()

        remote(istage, ibuf.at[b], is_.at[kk + 1], ir.at[kk + 1], yc_dev(2)).wait_recv()
        remote(qbuf.at[b], qbuf.at[b], qs.at[kk + 1], qr.at[kk + 1], yc_dev(2)).wait_recv()
        ts, ss = [], []
        for slot in (a, b):
            t, s = teacher(
                qbuf[slot], ibuf[slot, 0:1, :], ibuf[slot, 1:2, :], freq[...], kv[0], vt[...], eye[...]
            )
            ts.append(t)
            ss.append(s)
        gk, gv, d, t = student(
            jnp.concatenate(ss, axis=1), jnp.concatenate(ts, axis=1), pbuf[0], pbuf[1], pvt[...]
        )
        grad[0] += gk
        grad[1] += gv
        for n, slot in enumerate((a, b)):
            eout[slot, 0:1, :] = heads_sum(d[:, n * WIDE : (n + 1) * WIDE])
            eout[slot, 1:2, :] = heads_sum(t[:, n * WIDE : (n + 1) * WIDE])
        return carry

    lax.fori_loop(0, 4, body, 0)

    for k in PLANE:
        xx, zz = xz(k)
        src = grad.at[xx // 2, pl.ds(pl.multiple_of((xx % 2) * 64 + zz * 8, 8), 8)]
        remote(src, rland.at[k], gs, gr, xz_dev(k)).start()
    for k in range(1, 8):
        yy, cc = yc(k)
        cp = remote(eout.at[yy * 2 + cc], eland.at[head], es.at[k], er.at[k], yc_dev(k))
        cp.start()
        sent.append(cp)
    eland[head] = eout[head]
    rows8 = grad[x_hi, pl.ds(pl.multiple_of(x_lo * 64 + z * 8, 8), 8), :]
    all31 = rland.at[pl.ds(1, 31)]
    remote(all31, all31, gs, gr, xz_dev(1)).wait_recv()
    for k in range(1, 32):
        rows8 = rows8 + rland[k]
    own8[...] = rows8
    nsend[0:1] = jnp.sum(rows8 * rows8, axis=0, keepdims=True)
    ycs = []
    for k in (4, 5, 2, 3, 6, 7, 1):
        cp = remote(nsend.at[pl.ds(0, 1)], nyc.at[pl.ds(k, 1)], ns.at[0], nr.at[0], yc_dev(k))
        cp.start()

    @pl.when(jnp.logical_not(own_perm))
    def _():
        remote(own8, fin, ps.at[0], pr.at[0], perm_dev).start()

    @pl.when(own_perm)
    def _():
        fin[...] = own8[...]

    nyc[0:1] = nsend[0:1]
    seven = nyc.at[pl.ds(1, 7)]
    remote(seven, seven, ns.at[0], nr.at[0], yc_dev(1)).wait_recv()
    nsend[1:2] = jnp.sum(nyc[...], axis=0, keepdims=True)
    for k in PLANE:
        remote(nsend.at[pl.ds(1, 1)], nxz.at[pl.ds(k, 1)], ns.at[1], nr.at[1], xz_dev(k)).start()
    nxz[0:1] = nsend[1:2]
    for k in range(1, 8):
        remote(eout.at[k], eland.at[k], es.at[k], er.at[k], yc_dev(k)).wait_recv()
    esum = eland[0]
    for k in range(1, 8):
        esum = esum + eland[k]
    err_ref[...] = jnp.sqrt(esum[0:1] / FEATURES) / jnp.sqrt(esum[1:2] / FEATURES + norm_eps)
    for cp in sent:
        cp.wait_send()
    remote(all31, all31, gs, gr, xz_dev(1)).wait_send()
    remote(seven, seven, ns.at[0], nr.at[0], yc_dev(1)).wait_send()

    @pl.when(jnp.logical_not(own_perm))
    def _():
        remote(own8, fin, ps.at[0], pr.at[0], perm_dev).wait()

    thirty = nxz.at[pl.ds(1, 31)]
    remote(thirty, thirty, ns.at[1], nr.at[1], xz_dev(1)).wait()
    whole = jnp.sum(nxz[...], axis=0, keepdims=True)
    mean_square = jnp.sum(whole, axis=1, keepdims=True) / (2.0 * KVH * PRE * HD)
    step_ref[...] = fin[...] / jnp.sqrt(mean_square + norm_eps)


def frequencies():
    f = (rope_base ** (-np.arange(HD // 2, dtype=np.float64) / (HD // 2))).astype(np.float32)
    return np.broadcast_to(f[:, None], (HD // 2, ROWS)).copy()


def shards(queries, question_pos, cache_limit, cache, prefix):
    freq = jnp.asarray(frequencies())
    vmem = pl.BlockSpec(memory_space=pltpu.VMEM)
    hbm = pl.BlockSpec(memory_space=pltpu.HBM)
    f32, bf16 = jnp.float32, jnp.bfloat16
    dma = pltpu.SemaphoreType.DMA
    return pl.pallas_call(
        kernel,
        out_shape=(
            jax.ShapeDtypeStruct((8, HD), f32),
            jax.ShapeDtypeStruct((1, ROWS), f32),
        ),
        in_specs=[hbm] * 6,
        out_specs=(vmem, vmem),
        scratch_shapes=[
            pltpu.VMEM((8, ROWS, WIDE), bf16),
            pltpu.VMEM((8, 8, ROWS), jnp.int32),
            pltpu.VMEM((8, ROWS), jnp.int32),
            pltpu.VMEM((HD // 2, ROWS), f32),
            pltpu.VMEM((2, POS, HD), bf16),
            pltpu.VMEM((HD, POS), bf16),
            pltpu.VMEM((2, PRE, HD), bf16),
            pltpu.VMEM((HD, PRE), bf16),
            pltpu.VMEM((HD, HD), bf16),
            pltpu.VMEM((2, PRE, HD), f32),
            pltpu.VMEM((32, 8, HD), f32),
            pltpu.VMEM((8, HD), f32),
            pltpu.VMEM((8, 8, ROWS), f32),
            pltpu.VMEM((8, 8, ROWS), f32),
            pltpu.VMEM((8, HD), f32),
            pltpu.VMEM((8, HD), f32),
            pltpu.VMEM((32, HD), f32),
            pltpu.VMEM((8, HD), f32),
            dma((6,)),
            dma((8,)), dma((8,)), dma((8,)), dma((8,)), dma((8,)), dma((8,)), dma((8, 4)), dma((8, 4)),
            dma((8,)), dma((8,)), dma, dma, dma((1,)), dma((1,)), dma((2,)), dma((2,)),
        ],
        compiler_params=pltpu.CompilerParams(
            collective_id=0, has_side_effects=True, vmem_limit_bytes=60 * 1024 * 1024
        ),
        cost_estimate=pl.CostEstimate(
            flops=3_000_000_000, bytes_accessed=4_000_000, transcendentals=5_000_000
        ),
    )(queries, question_pos, cache_limit, cache, prefix, freq)


def solution(mesh):
    return jax.shard_map(
        shards,
        mesh=mesh,
        in_specs=(P("grp", "blk", None), P("grp", "blk"), P("grp", "blk"), P("blk", None), P()),
        out_specs=(P(("blk", "grp"), None), P("grp", "blk")),
        check_vma=False,
    )
```

```python
import math

import jax
import jax.numpy as jnp
import numpy as np
from jax import lax
from jax.experimental import pallas as pl
from jax.experimental.pallas import tpu as pltpu
from jax.sharding import PartitionSpec as P

MESH = pl.DeviceIdType.MESH
rope_base = 500000.0
neg_fill = -1e30
norm_eps = 1e-06

HD = 128
KVH = 8
PER = 4
ROWS = 128
POS = 1024
SHARD = 64
PRE = 128
FEATURES = KVH * PER * HD
WIDE = PER * HD
KEYS = KVH * HD
SCALE = HD**-0.5
JC = 256
SCALE_LOG2E = SCALE * math.log2(math.e)


def sincos(angle):
    k = jnp.floor(angle * (2.0 / math.pi) + 0.5)
    r = angle - k * 1.5703125
    r = r - k * 4.837512969970703125e-4
    r = r - k * 7.54978995489188216e-8
    r2 = r * r
    s = r + r * r2 * (-1.6666654611e-1 + r2 * (8.3321608736e-3 + r2 * -1.9515295891e-4))
    c = 1.0 + r2 * (
        -0.5 + r2 * (4.166664568298827e-2 + r2 * (-1.388731625493765e-3 + r2 * 2.443315711809948e-5))
    )
    n = k.astype(jnp.int32)
    odd = (n & 1) == 1
    sine = jnp.where(odd, c, s)
    cosine = jnp.where(odd, s, c)
    sine = jnp.where((n & 2) == 2, -sine, sine)
    cosine = jnp.where(((n + 1) & 2) == 2, -cosine, cosine)
    return sine, cosine


def dot(a, b, ca, cb):
    return lax.dot_general(a, b, (((ca,), (cb,)), ((), ())), preferred_element_type=jnp.float32)


def prepare(q, pos_row, lim_row, freq_col, eye):
    pos = pos_row.astype(jnp.float32)
    lim = lim_row.astype(jnp.float32)
    half = HD // 2
    st, ct = sincos(freq_col * (lim + pos))
    ss, cs = sincos(freq_col * (PRE + pos))
    tq, sq = [], []
    for h in range(PER):
        qt = dot(eye, q[:, h * HD : (h + 1) * HD], 1, 1)
        lead, trail = qt[:half], qt[half:]
        for cosine, sine, out in ((ct, st, tq), (cs, ss, sq)):
            out.append(
                jnp.concatenate(
                    [lead * cosine - trail * sine, trail * cosine + lead * sine], axis=0
                ).astype(jnp.bfloat16)
            )
    return jnp.concatenate(tq, axis=1), jnp.concatenate(sq, axis=1)


def teacher(tq, lim_row, keys, values_t):
    limits = jnp.concatenate([lim_row] * PER, axis=1)
    parts = []
    top = None
    for j in range(0, POS, JC):
        part = dot(keys[j : j + JC], tq, 1, 0)
        if j >= 256:
            where = lax.broadcasted_iota(jnp.int32, part.shape, 0) + j
            part = jnp.where(where < limits, part, neg_fill)
        parts.append(part)
        m = jnp.max(part, axis=0, keepdims=True)
        top = m if top is None else jnp.maximum(top, m)
    total = None
    mixture = None
    for a, part in enumerate(parts):
        e = jnp.exp2((part - top) * SCALE_LOG2E)
        t = jnp.sum(e, axis=0, keepdims=True)
        total = t if total is None else total + t
        o = dot(values_t[:, a * JC : (a + 1) * JC], e.astype(jnp.bfloat16), 1, 0)
        mixture = o if mixture is None else mixture + o
    return mixture * (1.0 / total)


def student_forward(sq, pk, pv_t):
    scores = dot(pk, sq, 1, 0)
    raised = jnp.exp2((scores - jnp.max(scores, axis=0, keepdims=True)) * SCALE_LOG2E)
    probs = raised * (1.0 / jnp.sum(raised, axis=0, keepdims=True))
    rounded = probs.astype(jnp.bfloat16)
    return probs, rounded, dot(pv_t, rounded, 1, 0)


def student_backward(sq, probs, rounded, out, target, pv):
    diff = out - target
    cot = diff.astype(jnp.bfloat16)
    along = dot(pv, cot, 1, 0)
    inner = jnp.sum(probs * along, axis=0, keepdims=True)
    grad = (probs * (along - inner) * SCALE).astype(jnp.bfloat16)
    gv = dot(rounded, cot, 1, 1)
    gk = dot(grad, sq, 1, 1)
    d = jnp.sum(diff * diff, axis=0, keepdims=True)
    t = jnp.sum(target * target, axis=0, keepdims=True)
    return gk, gv, d, t


def heads_sum(d):
    return d[:, :ROWS] + d[:, ROWS : 2 * ROWS] + d[:, 2 * ROWS : 3 * ROWS] + d[:, 3 * ROWS :]


HOPS = (0, 1, 2, 3, 4, 3, 2, 1)
PLANE = sorted(range(1, 32), key=lambda k: -(HOPS[k % 8] + (0, 1, 2, 1)[k // 8]))


def kernel(
    q_hbm, pos_hbm, lim_hbm, cache_hbm, prefix_hbm, freq_hbm,
    step_ref, err_ref,
    qbuf, ibuf, istage, freq, kv, vt, pbuf, pvt, eye, grad, rland, own8, eland, eout, nsend, nyc, nxz, fin,
    tqs, sqs, probs, rounded, outs,
    local_sem, qs, qr, is_, ir, zs, zr, fs, fr, es, er, gs, gr, ps, pr, ns, nr,
):
    blk, grp = lax.axis_index("blk"), lax.axis_index("grp")
    x_hi, z = blk // 8, blk % 8
    x_lo, head = grp // 8, grp % 8
    piece = x_hi * 16 + x_lo * 8 + z

    def yc_dev(k):
        return (blk, grp ^ k)

    def xz_dev(k):
        n = k // 8
        return (blk ^ ((n // 2) * 8 + k % 8), grp ^ ((n % 2) * 8) if n % 2 else grp)

    own_perm = z == head
    perm_dev = (x_hi * 8 + head, x_lo * 8 + z)

    def remote(src, dst, ssem, rsem, dev):
        return pltpu.make_async_remote_copy(
            src_ref=src, dst_ref=dst, send_sem=ssem, recv_sem=rsem,
            device_id=dev, device_id_type=MESH,
        )

    def cols(start, n):
        return pl.ds(pl.multiple_of(start, HD), n)

    def shard_rows(k):
        return pl.ds(pl.multiple_of((blk ^ k) * SHARD, SHARD), SHARD)

    def piece_rows(k):
        return pl.ds(pl.multiple_of((piece ^ k) * 8, 8), 8)

    barrier = pltpu.get_barrier_semaphore()
    for k in (4, 5, 3, 7, 2, 6, 1):
        pl.semaphore_signal(barrier, inc=1, device_id=xz_dev(k), device_id_type=MESH)
    for k in (16, 8, 24):
        pl.semaphore_signal(barrier, inc=1, device_id=xz_dev(k), device_id_type=MESH)
    for k in (4, 5, 2, 3, 6, 7, 1):
        pl.semaphore_signal(barrier, inc=1, device_id=yc_dev(k), device_id_type=MESH)

    own_rows = shard_rows(0)
    lc = [
        pltpu.make_async_copy(
            cache_hbm.at[:, cols(x_lo * KEYS + head * HD, HD)], kv.at[x_lo, own_rows], local_sem.at[0]
        ),
        pltpu.make_async_copy(pos_hbm, istage.at[pl.ds(0, 1)], local_sem.at[1]),
        pltpu.make_async_copy(lim_hbm, istage.at[pl.ds(1, 1)], local_sem.at[2]),
        pltpu.make_async_copy(q_hbm.at[0, :, cols(head * WIDE, WIDE)], qbuf.at[head], local_sem.at[3]),
        pltpu.make_async_copy(prefix_hbm.at[:, head], pbuf, local_sem.at[4]),
        pltpu.make_async_copy(freq_hbm, freq, local_sem.at[5]),
    ]
    for cp in lc:
        cp.start()
    eye[...] = jnp.where(
        lax.broadcasted_iota(jnp.int32, (HD, HD), 0) == lax.broadcasted_iota(jnp.int32, (HD, HD), 1), 1.0, 0.0
    ).astype(jnp.bfloat16)
    for cp in lc[:3]:
        cp.wait()

    pl.semaphore_wait(barrier, 17)

    sent = []
    zc = {}
    for k in (1, 7, 3, 2, 6, 5, 4):
        zc[k] = remote(kv.at[x_lo, own_rows], kv.at[x_lo, own_rows], zs.at[k], zr.at[k], xz_dev(k))
        zc[k].start()
        sent.append(zc[k])
    fc = []

    def forward(k):
        rows = shard_rows(k)
        for n in (2, 1, 3):
            cp = remote(kv.at[x_lo, rows], kv.at[x_lo, rows], fs.at[k, n], fr.at[k, n], xz_dev(8 * n))
            cp.start()
            fc.append(cp)
            sent.append(cp)

    qc = {}

    def send_rows(k):
        a = remote(istage, ibuf.at[head], is_.at[k], ir.at[k], yc_dev(k))
        a.start()
        b = remote(q_hbm.at[0, :, cols((head ^ k) * WIDE, WIDE)], qbuf.at[head], qs.at[k], qr.at[k], yc_dev(k))
        b.start()
        qc[k] = (a, b)
        sent.extend(qc[k])

    forward(0)
    for k in (1, 2, 3, 6, 7, 4, 5):
        send_rows(k)
    for k in (1, 7, 3, 2, 6, 5, 4):
        zc[k].wait_recv()
        forward(k)
    ibuf[head] = istage[...]
    for cp in lc[3:]:
        cp.wait()
    pvt[...] = pbuf[1].T

    def arrive(k):
        for cp in qc[k]:
            cp.wait_recv()

    def prep(i, k):
        s = head ^ k
        t, u = prepare(qbuf[s], ibuf[s, 0:1, :], ibuf[s, 1:2, :], freq[...], eye[...])
        tqs[:, i * WIDE : (i + 1) * WIDE] = t
        sqs[:, i * WIDE : (i + 1) * WIDE] = u

    def ahead():
        p, r, o = student_forward(sqs[...], pbuf[0], pvt[...])
        probs[...] = p
        rounded[...] = r
        outs[...] = o

    def rest(ks):
        target = jnp.concatenate(
            [
                teacher(tqs[:, i * WIDE : (i + 1) * WIDE], ibuf[head ^ k, 1:2, :], kv[0], vt[...])
                for i, k in enumerate(ks)
            ],
            axis=1,
        )
        gk, gv, d, t = student_backward(sqs[...], probs[...], rounded[...], outs[...], target, pbuf[1])
        for i, k in enumerate(ks):
            eout[head ^ k, 0:1, :] = heads_sum(d[:, i * WIDE : (i + 1) * WIDE])
            eout[head ^ k, 1:2, :] = heads_sum(t[:, i * WIDE : (i + 1) * WIDE])
        return gk, gv

    first, second = (0, 1, 2, 3), (6, 7, 4, 5)
    prep(0, 0)
    for i, k in enumerate(first[1:]):
        arrive(k)
        prep(i + 1, k)
    ahead()
    for cp in fc:
        cp.wait_recv()
    vt[...] = kv[1].T
    gk, gv = rest(first)
    grad[0:PRE] = gk
    grad[PRE:] = gv
    for k in second:
        arrive(k)
    for i, k in enumerate(second):
        prep(i, k)
    ahead()
    gk, gv = rest(second)
    grad[0:PRE] += gk
    grad[PRE:] += gv

    for k in PLANE:
        remote(grad.at[piece_rows(k)], rland.at[k], gs, gr, xz_dev(k)).start()
    for k in range(1, 8):
        cp = remote(eout.at[head ^ k], eland.at[head], es.at[k], er.at[k], yc_dev(k))
        cp.start()
        sent.append(cp)
    eland[head] = eout[head]
    rows8 = grad[piece_rows(0), :]
    all31 = rland.at[pl.ds(1, 31)]
    remote(all31, all31, gs, gr, xz_dev(1)).wait_recv()
    for k in range(1, 32):
        rows8 = rows8 + rland[k]
    own8[...] = rows8
    nsend[0:1] = jnp.sum(rows8 * rows8, axis=0, keepdims=True)
    for k in (4, 5, 2, 3, 6, 7, 1):
        remote(nsend.at[pl.ds(0, 1)], nyc.at[pl.ds(k, 1)], ns.at[0], nr.at[0], yc_dev(k)).start()

    @pl.when(jnp.logical_not(own_perm))
    def _():
        remote(own8, fin, ps.at[0], pr.at[0], perm_dev).start()

    @pl.when(own_perm)
    def _():
        fin[...] = own8[...]

    nyc[0:1] = nsend[0:1]
    seven = nyc.at[pl.ds(1, 7)]
    remote(seven, seven, ns.at[0], nr.at[0], yc_dev(1)).wait_recv()
    nsend[1:2] = jnp.sum(nyc[...], axis=0, keepdims=True)
    for k in PLANE:
        remote(nsend.at[pl.ds(1, 1)], nxz.at[pl.ds(k, 1)], ns.at[1], nr.at[1], xz_dev(k)).start()
    nxz[0:1] = nsend[1:2]
    for k in range(1, 8):
        remote(eout.at[k], eland.at[k], es.at[k], er.at[k], yc_dev(k)).wait_recv()
    esum = eland[0]
    for k in range(1, 8):
        esum = esum + eland[k]
    err_ref[...] = jnp.sqrt(esum[0:1] / FEATURES) / jnp.sqrt(esum[1:2] / FEATURES + norm_eps)
    for cp in sent:
        cp.wait_send()
    remote(all31, all31, gs, gr, xz_dev(1)).wait_send()
    remote(seven, seven, ns.at[0], nr.at[0], yc_dev(1)).wait_send()

    @pl.when(jnp.logical_not(own_perm))
    def _():
        remote(own8, fin, ps.at[0], pr.at[0], perm_dev).wait()

    thirty = nxz.at[pl.ds(1, 31)]
    remote(thirty, thirty, ns.at[1], nr.at[1], xz_dev(1)).wait()
    whole = jnp.sum(nxz[...], axis=0, keepdims=True)
    mean_square = jnp.sum(whole, axis=1, keepdims=True) / (2.0 * KVH * PRE * HD)
    step_ref[...] = fin[...] / jnp.sqrt(mean_square + norm_eps)


def frequencies():
    f = (rope_base ** (-np.arange(HD // 2, dtype=np.float64) / (HD // 2))).astype(np.float32)
    return np.broadcast_to(f[:, None], (HD // 2, ROWS)).copy()


def shards(queries, question_pos, cache_limit, cache, prefix):
    freq = jnp.asarray(frequencies())
    vmem = pl.BlockSpec(memory_space=pltpu.VMEM)
    hbm = pl.BlockSpec(memory_space=pltpu.HBM)
    f32, bf16 = jnp.float32, jnp.bfloat16
    dma = pltpu.SemaphoreType.DMA
    return pl.pallas_call(
        kernel,
        out_shape=(
            jax.ShapeDtypeStruct((8, HD), f32),
            jax.ShapeDtypeStruct((1, ROWS), f32),
        ),
        in_specs=[hbm] * 6,
        out_specs=(vmem, vmem),
        scratch_shapes=[
            pltpu.VMEM((8, ROWS, WIDE), bf16),
            pltpu.VMEM((8, 8, ROWS), jnp.int32),
            pltpu.VMEM((8, ROWS), jnp.int32),
            pltpu.VMEM((HD // 2, ROWS), f32),
            pltpu.VMEM((2, POS, HD), bf16),
            pltpu.VMEM((HD, POS), bf16),
            pltpu.VMEM((2, PRE, HD), bf16),
            pltpu.VMEM((HD, PRE), bf16),
            pltpu.VMEM((HD, HD), bf16),
            pltpu.VMEM((2 * PRE, HD), f32),
            pltpu.VMEM((32, 8, HD), f32),
            pltpu.VMEM((8, HD), f32),
            pltpu.VMEM((8, 8, ROWS), f32),
            pltpu.VMEM((8, 8, ROWS), f32),
            pltpu.VMEM((8, HD), f32),
            pltpu.VMEM((8, HD), f32),
            pltpu.VMEM((32, HD), f32),
            pltpu.VMEM((8, HD), f32),
            pltpu.VMEM((HD, 4 * WIDE), bf16),
            pltpu.VMEM((HD, 4 * WIDE), bf16),
            pltpu.VMEM((PRE, 4 * WIDE), f32),
            pltpu.VMEM((PRE, 4 * WIDE), bf16),
            pltpu.VMEM((HD, 4 * WIDE), f32),
            dma((6,)),
            dma((8,)), dma((8,)), dma((8,)), dma((8,)), dma((8,)), dma((8,)), dma((8, 4)), dma((8, 4)),
            dma((8,)), dma((8,)), dma, dma, dma((1,)), dma((1,)), dma((2,)), dma((2,)),
        ],
        compiler_params=pltpu.CompilerParams(
            collective_id=0, has_side_effects=True, vmem_limit_bytes=60 * 1024 * 1024
        ),
        cost_estimate=pl.CostEstimate(
            flops=3_000_000_000, bytes_accessed=4_000_000, transcendentals=5_000_000
        ),
    )(queries, question_pos, cache_limit, cache, prefix, freq)


def solution(mesh):
    return jax.shard_map(
        shards,
        mesh=mesh,
        in_specs=(P("grp", "blk", None), P("grp", "blk"), P("grp", "blk"), P("blk", None), P()),
        out_specs=(P(("blk", "grp"), None), P("grp", "blk")),
        check_vma=False,
    )
```

```python
import math

import jax
import jax.numpy as jnp
import numpy as np
from jax import lax
from jax.experimental import pallas as pl
from jax.experimental.pallas import tpu as pltpu
from jax.sharding import PartitionSpec as P

MESH = pl.DeviceIdType.MESH
rope_base = 500000.0
neg_fill = -1e30
norm_eps = 1e-06

HD = 128
KVH = 8
PER = 4
ROWS = 128
POS = 1024
SHARD = 64
PRE = 128
FEATURES = KVH * PER * HD
WIDE = PER * HD
KEYS = KVH * HD
SCALE = HD**-0.5
JC = 256
SCALE_LOG2E = SCALE * math.log2(math.e)


def sincos(angle):
    k = jnp.floor(angle * (2.0 / math.pi) + 0.5)
    r = angle - k * 1.5703125
    r = r - k * 4.837512969970703125e-4
    r = r - k * 7.54978995489188216e-8
    r2 = r * r
    s = r + r * r2 * (-1.6666654611e-1 + r2 * (8.3321608736e-3 + r2 * -1.9515295891e-4))
    c = 1.0 + r2 * (
        -0.5 + r2 * (4.166664568298827e-2 + r2 * (-1.388731625493765e-3 + r2 * 2.443315711809948e-5))
    )
    n = k.astype(jnp.int32)
    odd = (n & 1) == 1
    sine = jnp.where(odd, c, s)
    cosine = jnp.where(odd, s, c)
    sine = jnp.where((n & 2) == 2, -sine, sine)
    cosine = jnp.where(((n + 1) & 2) == 2, -cosine, cosine)
    return sine, cosine


def dot(a, b, ca, cb):
    return lax.dot_general(a, b, (((ca,), (cb,)), ((), ())), preferred_element_type=jnp.float32)


def prepare(q, pos_row, lim_row, freq_col, eye):
    pos = pos_row.astype(jnp.float32)
    lim = lim_row.astype(jnp.float32)
    half = HD // 2
    st, ct = sincos(freq_col * (lim + pos))
    ss, cs = sincos(freq_col * (PRE + pos))
    tq, sq = [], []
    for h in range(PER):
        qt = dot(eye, q[:, h * HD : (h + 1) * HD], 1, 1)
        lead, trail = qt[:half], qt[half:]
        for cosine, sine, out in ((ct, st, tq), (cs, ss, sq)):
            out.append(
                jnp.concatenate(
                    [lead * cosine - trail * sine, trail * cosine + lead * sine], axis=0
                ).astype(jnp.bfloat16)
            )
    return jnp.concatenate(tq, axis=1), jnp.concatenate(sq, axis=1)


def teacher(tq, lim_row, keys, values_t):
    limits = lim_row
    parts = []
    top = None
    for j in range(0, POS, JC):
        part = dot(keys[j : j + JC], tq, 1, 0)
        if j >= 256:
            where = lax.broadcasted_iota(jnp.int32, part.shape, 0) + j
            part = jnp.where(where < limits, part, neg_fill)
        parts.append(part)
        m = jnp.max(part, axis=0, keepdims=True)
        top = m if top is None else jnp.maximum(top, m)
    total = None
    mixture = None
    for a, part in enumerate(parts):
        e = jnp.exp2((part - top) * SCALE_LOG2E)
        t = jnp.sum(e, axis=0, keepdims=True)
        total = t if total is None else total + t
        o = dot(values_t[:, a * JC : (a + 1) * JC], e.astype(jnp.bfloat16), 1, 0)
        mixture = o if mixture is None else mixture + o
    return mixture * (1.0 / total)


def student_forward(sq, pk, pv_t):
    scores = dot(pk, sq, 1, 0)
    raised = jnp.exp2((scores - jnp.max(scores, axis=0, keepdims=True)) * SCALE_LOG2E)
    probs = raised * (1.0 / jnp.sum(raised, axis=0, keepdims=True))
    rounded = probs.astype(jnp.bfloat16)
    return probs, rounded, dot(pv_t, rounded, 1, 0)


def student_backward(sq, probs, rounded, out, target, pv):
    diff = out - target
    cot = diff.astype(jnp.bfloat16)
    along = dot(pv, cot, 1, 0)
    inner = jnp.sum(probs * along, axis=0, keepdims=True)
    grad = (probs * (along - inner) * SCALE).astype(jnp.bfloat16)
    gv = dot(rounded, cot, 1, 1)
    gk = dot(grad, sq, 1, 1)
    d = jnp.sum(diff * diff, axis=0, keepdims=True)
    t = jnp.sum(target * target, axis=0, keepdims=True)
    return gk, gv, d, t


def heads_sum(d):
    return d[:, :ROWS] + d[:, ROWS : 2 * ROWS] + d[:, 2 * ROWS : 3 * ROWS] + d[:, 3 * ROWS :]


HOPS = (0, 1, 2, 3, 4, 3, 2, 1)
PLANE = sorted(range(1, 32), key=lambda k: -(HOPS[k % 8] + (0, 1, 2, 1)[k // 8]))


def kernel(
    q_hbm, pos_hbm, lim_hbm, cache_hbm, prefix_hbm, freq_hbm,
    step_ref, err_ref,
    qbuf, ibuf, istage, freq, kv, vt, pbuf, pvt, eye, grad, rland, own8, eland, eout, nsend, nyc, nxz, fin,
    tqs, sqs, probs, rounded, outs,
    local_sem, qs, qr, is_, ir, zs, zr, fs, fr, es, er, gs, gr, ps, pr, ns, nr,
):
    blk, grp = lax.axis_index("blk"), lax.axis_index("grp")
    x_hi, z = blk // 8, blk % 8
    x_lo, head = grp // 8, grp % 8
    piece = x_hi * 16 + x_lo * 8 + z

    def yc_dev(k):
        return (blk, grp ^ k)

    def xz_dev(k):
        n = k // 8
        return (blk ^ ((n // 2) * 8 + k % 8), grp ^ ((n % 2) * 8) if n % 2 else grp)

    own_perm = z == head
    perm_dev = (x_hi * 8 + head, x_lo * 8 + z)

    def remote(src, dst, ssem, rsem, dev):
        return pltpu.make_async_remote_copy(
            src_ref=src, dst_ref=dst, send_sem=ssem, recv_sem=rsem,
            device_id=dev, device_id_type=MESH,
        )

    def cols(start, n):
        return pl.ds(pl.multiple_of(start, HD), n)

    def shard_rows(k):
        return pl.ds(pl.multiple_of((blk ^ k) * SHARD, SHARD), SHARD)

    def piece_rows(k):
        return pl.ds(pl.multiple_of((piece ^ k) * 8, 8), 8)

    barrier = pltpu.get_barrier_semaphore()
    for k in (4, 5, 3, 7, 2, 6, 1):
        pl.semaphore_signal(barrier, inc=1, device_id=xz_dev(k), device_id_type=MESH)
    for k in (16, 8, 24):
        pl.semaphore_signal(barrier, inc=1, device_id=xz_dev(k), device_id_type=MESH)
    for k in (4, 5, 2, 3, 6, 7, 1):
        pl.semaphore_signal(barrier, inc=1, device_id=yc_dev(k), device_id_type=MESH)

    own_rows = shard_rows(0)
    lc = [
        pltpu.make_async_copy(
            cache_hbm.at[:, cols(x_lo * KEYS + head * HD, HD)], kv.at[x_lo, own_rows], local_sem.at[0]
        ),
        pltpu.make_async_copy(pos_hbm, istage.at[pl.ds(0, 1)], local_sem.at[1]),
        pltpu.make_async_copy(lim_hbm, istage.at[pl.ds(1, 1)], local_sem.at[2]),
        pltpu.make_async_copy(q_hbm.at[0, :, cols(head * WIDE, WIDE)], qbuf.at[head], local_sem.at[3]),
        pltpu.make_async_copy(prefix_hbm.at[:, head], pbuf, local_sem.at[4]),
        pltpu.make_async_copy(freq_hbm, freq, local_sem.at[5]),
    ]
    for cp in lc:
        cp.start()
    eye[...] = jnp.where(
        lax.broadcasted_iota(jnp.int32, (HD, HD), 0) == lax.broadcasted_iota(jnp.int32, (HD, HD), 1), 1.0, 0.0
    ).astype(jnp.bfloat16)
    for cp in lc[:3]:
        cp.wait()

    pl.semaphore_wait(barrier, 17)

    sent = []
    zc = {}
    for k in (1, 7, 3, 2, 6, 5, 4):
        zc[k] = remote(kv.at[x_lo, own_rows], kv.at[x_lo, own_rows], zs.at[k], zr.at[k], xz_dev(k))
        zc[k].start()
        sent.append(zc[k])
    fc = []

    def forward(k):
        rows = shard_rows(k)
        for n in (2, 1, 3):
            cp = remote(kv.at[x_lo, rows], kv.at[x_lo, rows], fs.at[k, n], fr.at[k, n], xz_dev(8 * n))
            cp.start()
            fc.append(cp)
            sent.append(cp)

    qc = {}

    def send_rows(k):
        a = remote(istage, ibuf.at[head], is_.at[k], ir.at[k], yc_dev(k))
        a.start()
        b = remote(q_hbm.at[0, :, cols((head ^ k) * WIDE, WIDE)], qbuf.at[head], qs.at[k], qr.at[k], yc_dev(k))
        b.start()
        qc[k] = (a, b)
        sent.extend(qc[k])

    forward(0)
    for k in (1, 2, 3, 6, 7, 4, 5):
        send_rows(k)
    for k in (1, 7, 3, 2, 6, 5, 4):
        zc[k].wait_recv()
        forward(k)
    ibuf[head] = istage[...]
    for cp in lc[3:]:
        cp.wait()
    pvt[...] = pbuf[1].T

    def arrive(k):
        for cp in qc[k]:
            cp.wait_recv()

    def prep(i, k):
        s = head ^ k
        t, u = prepare(qbuf[s], ibuf[s, 0:1, :], ibuf[s, 1:2, :], freq[...], eye[...])
        tqs[:, i * WIDE : (i + 1) * WIDE] = t
        sqs[:, i * WIDE : (i + 1) * WIDE] = u

    def ahead():
        p, r, o = student_forward(sqs[...], pbuf[0], pvt[...])
        probs[...] = p
        rounded[...] = r
        outs[...] = o

    def rest(ks):
        target = jnp.concatenate(
            [
                teacher(
                    tqs[:, i * WIDE : (i + 2) * WIDE],
                    jnp.concatenate([ibuf[head ^ ks[i], 1:2, :]] * PER + [ibuf[head ^ ks[i + 1], 1:2, :]] * PER, axis=1),
                    kv[0],
                    vt[...],
                )
                for i in range(0, len(ks), 2)
            ],
            axis=1,
        )
        gk, gv, d, t = student_backward(sqs[...], probs[...], rounded[...], outs[...], target, pbuf[1])
        for i, k in enumerate(ks):
            eout[head ^ k, 0:1, :] = heads_sum(d[:, i * WIDE : (i + 1) * WIDE])
            eout[head ^ k, 1:2, :] = heads_sum(t[:, i * WIDE : (i + 1) * WIDE])
        return gk, gv

    first, second = (0, 1, 2, 3), (6, 7, 4, 5)
    prep(0, 0)
    for i, k in enumerate(first[1:]):
        arrive(k)
        prep(i + 1, k)
    ahead()
    for cp in fc:
        cp.wait_recv()
    vt[...] = kv[1].T
    gk, gv = rest(first)
    grad[0:PRE] = gk
    grad[PRE:] = gv
    for k in second:
        arrive(k)
    for i, k in enumerate(second):
        prep(i, k)
    ahead()
    gk, gv = rest(second)
    grad[0:PRE] += gk
    grad[PRE:] += gv

    for k in PLANE:
        remote(grad.at[piece_rows(k)], rland.at[k], gs, gr, xz_dev(k)).start()
    for k in range(1, 8):
        cp = remote(eout.at[head ^ k], eland.at[head], es.at[k], er.at[k], yc_dev(k))
        cp.start()
        sent.append(cp)
    eland[head] = eout[head]
    rows8 = grad[piece_rows(0), :]
    all31 = rland.at[pl.ds(1, 31)]
    remote(all31, all31, gs, gr, xz_dev(1)).wait_recv()
    for k in range(1, 32):
        rows8 = rows8 + rland[k]
    own8[...] = rows8
    nsend[0:1] = jnp.sum(rows8 * rows8, axis=0, keepdims=True)
    for k in (4, 5, 2, 3, 6, 7, 1):
        remote(nsend.at[pl.ds(0, 1)], nyc.at[pl.ds(k, 1)], ns.at[0], nr.at[0], yc_dev(k)).start()

    @pl.when(jnp.logical_not(own_perm))
    def _():
        remote(own8, fin, ps.at[0], pr.at[0], perm_dev).start()

    @pl.when(own_perm)
    def _():
        fin[...] = own8[...]

    nyc[0:1] = nsend[0:1]
    seven = nyc.at[pl.ds(1, 7)]
    remote(seven, seven, ns.at[0], nr.at[0], yc_dev(1)).wait_recv()
    nsend[1:2] = jnp.sum(nyc[...], axis=0, keepdims=True)
    for k in PLANE:
        remote(nsend.at[pl.ds(1, 1)], nxz.at[pl.ds(k, 1)], ns.at[1], nr.at[1], xz_dev(k)).start()
    nxz[0:1] = nsend[1:2]
    for k in range(1, 8):
        remote(eout.at[k], eland.at[k], es.at[k], er.at[k], yc_dev(k)).wait_recv()
    esum = eland[0]
    for k in range(1, 8):
        esum = esum + eland[k]
    err_ref[...] = jnp.sqrt(esum[0:1] / FEATURES) / jnp.sqrt(esum[1:2] / FEATURES + norm_eps)
    for cp in sent:
        cp.wait_send()
    remote(all31, all31, gs, gr, xz_dev(1)).wait_send()
    remote(seven, seven, ns.at[0], nr.at[0], yc_dev(1)).wait_send()

    @pl.when(jnp.logical_not(own_perm))
    def _():
        remote(own8, fin, ps.at[0], pr.at[0], perm_dev).wait()

    thirty = nxz.at[pl.ds(1, 31)]
    remote(thirty, thirty, ns.at[1], nr.at[1], xz_dev(1)).wait()
    whole = jnp.sum(nxz[...], axis=0, keepdims=True)
    mean_square = jnp.sum(whole, axis=1, keepdims=True) / (2.0 * KVH * PRE * HD)
    step_ref[...] = fin[...] / jnp.sqrt(mean_square + norm_eps)


def frequencies():
    f = (rope_base ** (-np.arange(HD // 2, dtype=np.float64) / (HD // 2))).astype(np.float32)
    return np.broadcast_to(f[:, None], (HD // 2, ROWS)).copy()


def shards(queries, question_pos, cache_limit, cache, prefix):
    freq = jnp.asarray(frequencies())
    vmem = pl.BlockSpec(memory_space=pltpu.VMEM)
    hbm = pl.BlockSpec(memory_space=pltpu.HBM)
    f32, bf16 = jnp.float32, jnp.bfloat16
    dma = pltpu.SemaphoreType.DMA
    return pl.pallas_call(
        kernel,
        out_shape=(
            jax.ShapeDtypeStruct((8, HD), f32),
            jax.ShapeDtypeStruct((1, ROWS), f32),
        ),
        in_specs=[hbm] * 6,
        out_specs=(vmem, vmem),
        scratch_shapes=[
            pltpu.VMEM((8, ROWS, WIDE), bf16),
            pltpu.VMEM((8, 8, ROWS), jnp.int32),
            pltpu.VMEM((8, ROWS), jnp.int32),
            pltpu.VMEM((HD // 2, ROWS), f32),
            pltpu.VMEM((2, POS, HD), bf16),
            pltpu.VMEM((HD, POS), bf16),
            pltpu.VMEM((2, PRE, HD), bf16),
            pltpu.VMEM((HD, PRE), bf16),
            pltpu.VMEM((HD, HD), bf16),
            pltpu.VMEM((2 * PRE, HD), f32),
            pltpu.VMEM((32, 8, HD), f32),
            pltpu.VMEM((8, HD), f32),
            pltpu.VMEM((8, 8, ROWS), f32),
            pltpu.VMEM((8, 8, ROWS), f32),
            pltpu.VMEM((8, HD), f32),
            pltpu.VMEM((8, HD), f32),
            pltpu.VMEM((32, HD), f32),
            pltpu.VMEM((8, HD), f32),
            pltpu.VMEM((HD, 4 * WIDE), bf16),
            pltpu.VMEM((HD, 4 * WIDE), bf16),
            pltpu.VMEM((PRE, 4 * WIDE), f32),
            pltpu.VMEM((PRE, 4 * WIDE), bf16),
            pltpu.VMEM((HD, 4 * WIDE), f32),
            dma((6,)),
            dma((8,)), dma((8,)), dma((8,)), dma((8,)), dma((8,)), dma((8,)), dma((8, 4)), dma((8, 4)),
            dma((8,)), dma((8,)), dma, dma, dma((1,)), dma((1,)), dma((2,)), dma((2,)),
        ],
        compiler_params=pltpu.CompilerParams(
            collective_id=0, has_side_effects=True, vmem_limit_bytes=60 * 1024 * 1024
        ),
        cost_estimate=pl.CostEstimate(
            flops=3_000_000_000, bytes_accessed=4_000_000, transcendentals=5_000_000
        ),
    )(queries, question_pos, cache_limit, cache, prefix, freq)


def solution(mesh):
    return jax.shard_map(
        shards,
        mesh=mesh,
        in_specs=(P("grp", "blk", None), P("grp", "blk"), P("grp", "blk"), P("blk", None), P()),
        out_specs=(P(("blk", "grp"), None), P("grp", "blk")),
        check_vma=False,
    )
```

```python
import math

import jax
import jax.numpy as jnp
import numpy as np
from jax import lax
from jax.experimental import pallas as pl
from jax.experimental.pallas import tpu as pltpu
from jax.sharding import PartitionSpec as P

MESH = pl.DeviceIdType.MESH
rope_base = 500000.0
neg_fill = -1e30
norm_eps = 1e-06

HD = 128
KVH = 8
PER = 4
ROWS = 128
POS = 1024
SHARD = 64
PRE = 128
FEATURES = KVH * PER * HD
WIDE = PER * HD
KEYS = KVH * HD
SCALE = HD**-0.5
JC = 256
SCALE_LOG2E = SCALE * math.log2(math.e)


def sincos(angle):
    k = jnp.floor(angle * (2.0 / math.pi) + 0.5)
    r = angle - k * 1.5703125
    r = r - k * 4.837512969970703125e-4
    r = r - k * 7.54978995489188216e-8
    r2 = r * r
    s = r + r * r2 * (-1.6666654611e-1 + r2 * (8.3321608736e-3 + r2 * -1.9515295891e-4))
    c = 1.0 + r2 * (
        -0.5 + r2 * (4.166664568298827e-2 + r2 * (-1.388731625493765e-3 + r2 * 2.443315711809948e-5))
    )
    n = k.astype(jnp.int32)
    odd = (n & 1) == 1
    sine = jnp.where(odd, c, s)
    cosine = jnp.where(odd, s, c)
    sine = jnp.where((n & 2) == 2, -sine, sine)
    cosine = jnp.where(((n + 1) & 2) == 2, -cosine, cosine)
    return sine, cosine


def dot(a, b, ca, cb):
    return lax.dot_general(a, b, (((ca,), (cb,)), ((), ())), preferred_element_type=jnp.float32)


def prepare(q, pos_row, lim_row, freq_col, eye):
    pos = pos_row.astype(jnp.float32)
    lim = lim_row.astype(jnp.float32)
    half = HD // 2
    st, ct = sincos(freq_col * (lim + pos))
    ss, cs = sincos(freq_col * (PRE + pos))
    tq, sq = [], []
    for h in range(PER):
        qt = dot(eye, q[:, h * HD : (h + 1) * HD], 1, 1)
        lead, trail = qt[:half], qt[half:]
        for cosine, sine, out in ((ct, st, tq), (cs, ss, sq)):
            out.append(
                jnp.concatenate(
                    [lead * cosine - trail * sine, trail * cosine + lead * sine], axis=0
                ).astype(jnp.bfloat16)
            )
    return jnp.concatenate(tq, axis=1), jnp.concatenate(sq, axis=1)


def teacher(tq, lim_row, keys, values_t):
    limits = lim_row
    parts = []
    top = None
    for j in range(0, POS, JC):
        part = dot(keys[j : j + JC], tq, 1, 0)
        if j >= 256:
            where = lax.broadcasted_iota(jnp.int32, part.shape, 0) + j
            part = jnp.where(where < limits, part, neg_fill)
        parts.append(part)
        m = jnp.max(part, axis=0, keepdims=True)
        top = m if top is None else jnp.maximum(top, m)
    total = None
    mixture = None
    for a, part in enumerate(parts):
        e = jnp.exp2((part - top) * SCALE_LOG2E)
        t = jnp.sum(e, axis=0, keepdims=True)
        total = t if total is None else total + t
        o = dot(values_t[:, a * JC : (a + 1) * JC], e.astype(jnp.bfloat16), 1, 0)
        mixture = o if mixture is None else mixture + o
    return mixture * (1.0 / total)


def student_forward(sq, pk, pv_t):
    scores = dot(pk, sq, 1, 0)
    raised = jnp.exp2((scores - jnp.max(scores, axis=0, keepdims=True)) * SCALE_LOG2E)
    probs = raised * (1.0 / jnp.sum(raised, axis=0, keepdims=True))
    rounded = probs.astype(jnp.bfloat16)
    return probs, rounded, dot(pv_t, rounded, 1, 0)


def student_backward(sq, probs, rounded, out, target, pv):
    diff = out - target
    cot = diff.astype(jnp.bfloat16)
    along = dot(pv, cot, 1, 0)
    inner = jnp.sum(probs * along, axis=0, keepdims=True)
    grad = (probs * (along - inner) * SCALE).astype(jnp.bfloat16)
    gv = dot(rounded, cot, 1, 1)
    gk = dot(grad, sq, 1, 1)
    d = jnp.sum(diff * diff, axis=0, keepdims=True)
    t = jnp.sum(target * target, axis=0, keepdims=True)
    return gk, gv, d, t


def heads_sum(d):
    return d[:, :ROWS] + d[:, ROWS : 2 * ROWS] + d[:, 2 * ROWS : 3 * ROWS] + d[:, 3 * ROWS :]


HOPS = (0, 1, 2, 3, 4, 3, 2, 1)
PLANE = sorted(range(1, 32), key=lambda k: -(HOPS[k % 8] + (0, 1, 2, 1)[k // 8]))


def kernel(
    q_hbm, pos_hbm, lim_hbm, cache_hbm, prefix_hbm, freq_hbm,
    step_ref, err_ref,
    qbuf, ibuf, istage, freq, kv, vt, pbuf, pvt, eye, grad, rland, own8, eland, eout, nsend, nyc, nxz, fin,
    tqs, sqs, probs, rounded, outs,
    local_sem, qs, qr, is_, ir, zs, zr, fs, fr, es, er, gs, gr, ps, pr, ns, nr,
):
    blk, grp = lax.axis_index("blk"), lax.axis_index("grp")
    x_hi, z = blk // 8, blk % 8
    x_lo, head = grp // 8, grp % 8
    piece = x_hi * 16 + x_lo * 8 + z

    def yc_dev(k):
        return (blk, grp ^ k)

    def xz_dev(k):
        n = k // 8
        return (blk ^ ((n // 2) * 8 + k % 8), grp ^ ((n % 2) * 8) if n % 2 else grp)

    own_perm = z == head
    perm_dev = (x_hi * 8 + head, x_lo * 8 + z)

    def remote(src, dst, ssem, rsem, dev):
        return pltpu.make_async_remote_copy(
            src_ref=src, dst_ref=dst, send_sem=ssem, recv_sem=rsem,
            device_id=dev, device_id_type=MESH,
        )

    def cols(start, n):
        return pl.ds(pl.multiple_of(start, HD), n)

    def shard_rows(k):
        return pl.ds(pl.multiple_of((blk ^ k) * SHARD, SHARD), SHARD)

    def piece_rows(k):
        return pl.ds(pl.multiple_of((piece ^ k) * 8, 8), 8)

    barrier = pltpu.get_barrier_semaphore()
    for k in (4, 5, 3, 7, 2, 6, 1):
        pl.semaphore_signal(barrier, inc=1, device_id=xz_dev(k), device_id_type=MESH)
    for k in (16, 8, 24):
        pl.semaphore_signal(barrier, inc=1, device_id=xz_dev(k), device_id_type=MESH)
    for k in (4, 5, 2, 3, 6, 7, 1):
        pl.semaphore_signal(barrier, inc=1, device_id=yc_dev(k), device_id_type=MESH)

    own_rows = shard_rows(0)
    lc = [
        pltpu.make_async_copy(
            cache_hbm.at[:, cols(x_lo * KEYS + head * HD, HD)], kv.at[x_lo, own_rows], local_sem.at[0]
        ),
        pltpu.make_async_copy(pos_hbm, istage.at[pl.ds(0, 1)], local_sem.at[1]),
        pltpu.make_async_copy(lim_hbm, istage.at[pl.ds(1, 1)], local_sem.at[2]),
        pltpu.make_async_copy(q_hbm.at[0, :, cols(head * WIDE, WIDE)], qbuf.at[head], local_sem.at[3]),
        pltpu.make_async_copy(prefix_hbm.at[:, head], pbuf, local_sem.at[4]),
        pltpu.make_async_copy(freq_hbm, freq, local_sem.at[5]),
    ]
    for cp in lc:
        cp.start()
    eye[...] = jnp.where(
        lax.broadcasted_iota(jnp.int32, (HD, HD), 0) == lax.broadcasted_iota(jnp.int32, (HD, HD), 1), 1.0, 0.0
    ).astype(jnp.bfloat16)
    for cp in lc[:3]:
        cp.wait()

    pl.semaphore_wait(barrier, 17)

    sent = []
    zc = {}
    for k in (1, 7, 3, 2, 6, 5, 4):
        zc[k] = remote(kv.at[x_lo, own_rows], kv.at[x_lo, own_rows], zs.at[k], zr.at[k], xz_dev(k))
        zc[k].start()
        sent.append(zc[k])
    fc = []

    def forward(k):
        rows = shard_rows(k)
        for n in (2, 1, 3):
            cp = remote(kv.at[x_lo, rows], kv.at[x_lo, rows], fs.at[k, n], fr, xz_dev(8 * n))
            cp.start()
            fc.append(cp)
            sent.append(cp)

    qc = {}

    def send_rows(k):
        a = remote(istage, ibuf.at[head], is_.at[k], ir.at[k], yc_dev(k))
        a.start()
        b = remote(q_hbm.at[0, :, cols((head ^ k) * WIDE, WIDE)], qbuf.at[head], qs.at[k], qr.at[k], yc_dev(k))
        b.start()
        qc[k] = (a, b)
        sent.extend(qc[k])

    forward(0)
    for k in (1, 2, 3, 6, 7, 4, 5):
        send_rows(k)
    for k in (1, 7, 3, 2, 6, 5, 4):
        zc[k].wait_recv()
        forward(k)
    ibuf[head] = istage[...]
    for cp in lc[3:]:
        cp.wait()
    pvt[...] = pbuf[1].T

    def arrive(k):
        for cp in qc[k]:
            cp.wait_recv()

    def prep(i, k):
        s = head ^ k
        t, u = prepare(qbuf[s], ibuf[s, 0:1, :], ibuf[s, 1:2, :], freq[...], eye[...])
        tqs[:, i * WIDE : (i + 1) * WIDE] = t
        sqs[:, i * WIDE : (i + 1) * WIDE] = u

    def ahead():
        p, r, o = student_forward(sqs[...], pbuf[0], pvt[...])
        probs[...] = p
        rounded[...] = r
        outs[...] = o

    def rest(ks):
        target = jnp.concatenate(
            [
                teacher(
                    tqs[:, i * WIDE : (i + 2) * WIDE],
                    jnp.concatenate([ibuf[head ^ ks[i], 1:2, :]] * PER + [ibuf[head ^ ks[i + 1], 1:2, :]] * PER, axis=1),
                    kv[0],
                    vt[...],
                )
                for i in range(0, len(ks), 2)
            ],
            axis=1,
        )
        gk, gv, d, t = student_backward(sqs[...], probs[...], rounded[...], outs[...], target, pbuf[1])
        for i, k in enumerate(ks):
            eout[head ^ k, 0:1, :] = heads_sum(d[:, i * WIDE : (i + 1) * WIDE])
            eout[head ^ k, 1:2, :] = heads_sum(t[:, i * WIDE : (i + 1) * WIDE])
        return gk, gv

    first, second = (0, 1, 2, 3), (6, 7, 4, 5)
    prep(0, 0)
    for i, k in enumerate(first[1:]):
        arrive(k)
        prep(i + 1, k)
    ahead()
    three = qbuf.at[pl.ds(0, 3)]
    remote(three, three, fs.at[0, 1], fr, xz_dev(8)).wait_recv()
    vt[...] = kv[1].T
    gk, gv = rest(first)
    grad[0:PRE] = gk
    grad[PRE:] = gv
    for k in second:
        arrive(k)
    for i, k in enumerate(second):
        prep(i, k)
    ahead()
    gk, gv = rest(second)
    grad[0:PRE] += gk
    grad[PRE:] += gv

    for k in PLANE:
        remote(grad.at[piece_rows(k)], rland.at[k], gs, gr, xz_dev(k)).start()
    for k in range(1, 8):
        cp = remote(eout.at[head ^ k], eland.at[head], es.at[k], er.at[k], yc_dev(k))
        cp.start()
        sent.append(cp)
    eland[head] = eout[head]
    rows8 = grad[piece_rows(0), :]
    all31 = rland.at[pl.ds(1, 31)]
    remote(all31, all31, gs, gr, xz_dev(1)).wait_recv()
    for k in range(1, 32):
        rows8 = rows8 + rland[k]
    own8[...] = rows8
    nsend[0:1] = jnp.sum(rows8 * rows8, axis=0, keepdims=True)
    for k in (4, 5, 2, 3, 6, 7, 1):
        remote(nsend.at[pl.ds(0, 1)], nyc.at[pl.ds(k, 1)], ns.at[0], nr.at[0], yc_dev(k)).start()

    @pl.when(jnp.logical_not(own_perm))
    def _():
        remote(own8, fin, ps.at[0], pr.at[0], perm_dev).start()

    @pl.when(own_perm)
    def _():
        fin[...] = own8[...]

    nyc[0:1] = nsend[0:1]
    seven = nyc.at[pl.ds(1, 7)]
    remote(seven, seven, ns.at[0], nr.at[0], yc_dev(1)).wait_recv()
    nsend[1:2] = jnp.sum(nyc[...], axis=0, keepdims=True)
    for k in PLANE:
        remote(nsend.at[pl.ds(1, 1)], nxz.at[pl.ds(k, 1)], ns.at[1], nr.at[1], xz_dev(k)).start()
    nxz[0:1] = nsend[1:2]
    for k in range(1, 8):
        remote(eout.at[k], eland.at[k], es.at[k], er.at[k], yc_dev(k)).wait_recv()
    esum = eland[0]
    for k in range(1, 8):
        esum = esum + eland[k]
    err_ref[...] = jnp.sqrt(esum[0:1] / FEATURES) / jnp.sqrt(esum[1:2] / FEATURES + norm_eps)
    for cp in sent:
        cp.wait_send()
    remote(all31, all31, gs, gr, xz_dev(1)).wait_send()
    remote(seven, seven, ns.at[0], nr.at[0], yc_dev(1)).wait_send()

    @pl.when(jnp.logical_not(own_perm))
    def _():
        remote(own8, fin, ps.at[0], pr.at[0], perm_dev).wait()

    thirty = nxz.at[pl.ds(1, 31)]
    remote(thirty, thirty, ns.at[1], nr.at[1], xz_dev(1)).wait()
    whole = jnp.sum(nxz[...], axis=0, keepdims=True)
    mean_square = jnp.sum(whole, axis=1, keepdims=True) / (2.0 * KVH * PRE * HD)
    step_ref[...] = fin[...] / jnp.sqrt(mean_square + norm_eps)


def frequencies():
    f = (rope_base ** (-np.arange(HD // 2, dtype=np.float64) / (HD // 2))).astype(np.float32)
    return np.broadcast_to(f[:, None], (HD // 2, ROWS)).copy()


def shards(queries, question_pos, cache_limit, cache, prefix):
    freq = jnp.asarray(frequencies())
    vmem = pl.BlockSpec(memory_space=pltpu.VMEM)
    hbm = pl.BlockSpec(memory_space=pltpu.HBM)
    f32, bf16 = jnp.float32, jnp.bfloat16
    dma = pltpu.SemaphoreType.DMA
    return pl.pallas_call(
        kernel,
        out_shape=(
            jax.ShapeDtypeStruct((8, HD), f32),
            jax.ShapeDtypeStruct((1, ROWS), f32),
        ),
        in_specs=[hbm] * 6,
        out_specs=(vmem, vmem),
        scratch_shapes=[
            pltpu.VMEM((8, ROWS, WIDE), bf16),
            pltpu.VMEM((8, 8, ROWS), jnp.int32),
            pltpu.VMEM((8, ROWS), jnp.int32),
            pltpu.VMEM((HD // 2, ROWS), f32),
            pltpu.VMEM((2, POS, HD), bf16),
            pltpu.VMEM((HD, POS), bf16),
            pltpu.VMEM((2, PRE, HD), bf16),
            pltpu.VMEM((HD, PRE), bf16),
            pltpu.VMEM((HD, HD), bf16),
            pltpu.VMEM((2 * PRE, HD), f32),
            pltpu.VMEM((32, 8, HD), f32),
            pltpu.VMEM((8, HD), f32),
            pltpu.VMEM((8, 8, ROWS), f32),
            pltpu.VMEM((8, 8, ROWS), f32),
            pltpu.VMEM((8, HD), f32),
            pltpu.VMEM((8, HD), f32),
            pltpu.VMEM((32, HD), f32),
            pltpu.VMEM((8, HD), f32),
            pltpu.VMEM((HD, 4 * WIDE), bf16),
            pltpu.VMEM((HD, 4 * WIDE), bf16),
            pltpu.VMEM((PRE, 4 * WIDE), f32),
            pltpu.VMEM((PRE, 4 * WIDE), bf16),
            pltpu.VMEM((HD, 4 * WIDE), f32),
            dma((6,)),
            dma((8,)), dma((8,)), dma((8,)), dma((8,)), dma((8,)), dma((8,)), dma((8, 4)), dma,
            dma((8,)), dma((8,)), dma, dma, dma((1,)), dma((1,)), dma((2,)), dma((2,)),
        ],
        compiler_params=pltpu.CompilerParams(
            collective_id=0, has_side_effects=True, vmem_limit_bytes=60 * 1024 * 1024
        ),
        cost_estimate=pl.CostEstimate(
            flops=3_000_000_000, bytes_accessed=4_000_000, transcendentals=5_000_000
        ),
    )(queries, question_pos, cache_limit, cache, prefix, freq)


def solution(mesh):
    return jax.shard_map(
        shards,
        mesh=mesh,
        in_specs=(P("grp", "blk", None), P("grp", "blk"), P("grp", "blk"), P("blk", None), P()),
        out_specs=(P(("blk", "grp"), None), P("grp", "blk")),
        check_vma=False,
    )
```

```python
import math

import jax
import jax.numpy as jnp
import numpy as np
from jax import lax
from jax.experimental import pallas as pl
from jax.experimental.pallas import tpu as pltpu
from jax.sharding import PartitionSpec as P

MESH = pl.DeviceIdType.MESH
rope_base = 500000.0
neg_fill = -1e30
norm_eps = 1e-06

HD = 128
KVH = 8
PER = 4
ROWS = 128
POS = 1024
SHARD = 64
PRE = 128
FEATURES = KVH * PER * HD
WIDE = PER * HD
KEYS = KVH * HD
SCALE = HD**-0.5
JC = 256
SCALE_LOG2E = SCALE * math.log2(math.e)


def sincos(angle):
    k = jnp.floor(angle * (2.0 / math.pi) + 0.5)
    r = angle - k * 1.5703125
    r = r - k * 4.837512969970703125e-4
    r = r - k * 7.54978995489188216e-8
    r2 = r * r
    s = r + r * r2 * (-1.6666654611e-1 + r2 * (8.3321608736e-3 + r2 * -1.9515295891e-4))
    c = 1.0 + r2 * (
        -0.5 + r2 * (4.166664568298827e-2 + r2 * (-1.388731625493765e-3 + r2 * 2.443315711809948e-5))
    )
    n = k.astype(jnp.int32)
    odd = (n & 1) == 1
    sine = jnp.where(odd, c, s)
    cosine = jnp.where(odd, s, c)
    sine = jnp.where((n & 2) == 2, -sine, sine)
    cosine = jnp.where(((n + 1) & 2) == 2, -cosine, cosine)
    return sine, cosine


def dot(a, b, ca, cb):
    return lax.dot_general(a, b, (((ca,), (cb,)), ((), ())), preferred_element_type=jnp.float32)


def prepare(q, pos_row, lim_row, freq_col, eye):
    pos = pos_row.astype(jnp.float32)
    lim = lim_row.astype(jnp.float32)
    half = HD // 2
    st, ct = sincos(freq_col * (lim + pos))
    ss, cs = sincos(freq_col * (PRE + pos))
    tq, sq = [], []
    for h in range(PER):
        qt = dot(eye, q[:, h * HD : (h + 1) * HD], 1, 1)
        lead, trail = qt[:half], qt[half:]
        for cosine, sine, out in ((ct, st, tq), (cs, ss, sq)):
            out.append(
                jnp.concatenate(
                    [lead * cosine - trail * sine, trail * cosine + lead * sine], axis=0
                ).astype(jnp.bfloat16)
            )
    return jnp.concatenate(tq, axis=1), jnp.concatenate(sq, axis=1)


def teacher(tq, lim_row, keys, values_t):
    limits = lim_row
    parts = []
    top = None
    for j in range(0, POS, JC):
        part = dot(keys[j : j + JC], tq, 1, 0)
        if j >= 256:
            where = lax.broadcasted_iota(jnp.int32, part.shape, 0) + j
            part = jnp.where(where < limits, part, neg_fill)
        parts.append(part)
        m = jnp.max(part, axis=0, keepdims=True)
        top = m if top is None else jnp.maximum(top, m)
    total = None
    mixture = None
    for a, part in enumerate(parts):
        e = jnp.exp2((part - top) * SCALE_LOG2E)
        t = jnp.sum(e, axis=0, keepdims=True)
        total = t if total is None else total + t
        o = dot(values_t[:, a * JC : (a + 1) * JC], e.astype(jnp.bfloat16), 1, 0)
        mixture = o if mixture is None else mixture + o
    return mixture * (1.0 / total)


def student_forward(sq, pk, pv_t):
    scores = dot(pk, sq, 1, 0)
    raised = jnp.exp2((scores - jnp.max(scores, axis=0, keepdims=True)) * SCALE_LOG2E)
    probs = raised * (1.0 / jnp.sum(raised, axis=0, keepdims=True))
    rounded = probs.astype(jnp.bfloat16)
    return probs, rounded, dot(pv_t, rounded, 1, 0)


def student_backward(sq, probs, rounded, out, target, pv):
    diff = out - target
    cot = diff.astype(jnp.bfloat16)
    along = dot(pv, cot, 1, 0)
    inner = jnp.sum(probs * along, axis=0, keepdims=True)
    grad = (probs * (along - inner) * SCALE).astype(jnp.bfloat16)
    gv = dot(rounded, cot, 1, 1)
    gk = dot(grad, sq, 1, 1)
    d = jnp.sum(diff * diff, axis=0, keepdims=True)
    t = jnp.sum(target * target, axis=0, keepdims=True)
    return gk, gv, d, t


def heads_sum(d):
    return d[:, :ROWS] + d[:, ROWS : 2 * ROWS] + d[:, 2 * ROWS : 3 * ROWS] + d[:, 3 * ROWS :]


HOPS = (0, 1, 2, 3, 4, 3, 2, 1)
PLANE = sorted(range(1, 32), key=lambda k: -(HOPS[k % 8] + (0, 1, 2, 1)[k // 8]))


def kernel(
    q_hbm, pos_hbm, lim_hbm, cache_hbm, prefix_hbm, freq_hbm,
    step_ref, err_ref,
    qbuf, ibuf, istage, freq, kv, vt, pbuf, pvt, eye, grad, rland, own8, eland, eout, nsend, nyc, nxz, fin,
    tqs, sqs, probs, rounded, outs,
    local_sem, qs, qr, is_, ir, zs, zr, fs, fr, es, er, gs, gr, ps, pr, ns, nr,
):
    blk, grp = lax.axis_index("blk"), lax.axis_index("grp")
    x_hi, z = blk // 8, blk % 8
    x_lo, head = grp // 8, grp % 8
    piece = x_hi * 16 + x_lo * 8 + z

    def yc_dev(k):
        return (blk, grp ^ k)

    def xz_dev(k):
        n = k // 8
        return (blk ^ ((n // 2) * 8 + k % 8), grp ^ ((n % 2) * 8) if n % 2 else grp)

    own_perm = z == head
    perm_dev = (x_hi * 8 + head, x_lo * 8 + z)

    def remote(src, dst, ssem, rsem, dev):
        return pltpu.make_async_remote_copy(
            src_ref=src, dst_ref=dst, send_sem=ssem, recv_sem=rsem,
            device_id=dev, device_id_type=MESH,
        )

    def cols(start, n):
        return pl.ds(pl.multiple_of(start, HD), n)

    def shard_rows(k):
        return pl.ds(pl.multiple_of((blk ^ k) * SHARD, SHARD), SHARD)

    def piece_rows(k):
        return pl.ds(pl.multiple_of((piece ^ k) * 8, 8), 8)

    barrier = pltpu.get_barrier_semaphore()
    for k in (4, 5, 3, 7, 2, 6, 1):
        pl.semaphore_signal(barrier, inc=1, device_id=xz_dev(k), device_id_type=MESH)
    for k in (16, 8, 24):
        pl.semaphore_signal(barrier, inc=1, device_id=xz_dev(k), device_id_type=MESH)
    for k in (4, 5, 2, 3, 6, 7, 1):
        pl.semaphore_signal(barrier, inc=1, device_id=yc_dev(k), device_id_type=MESH)

    own_rows = shard_rows(0)
    lc = [
        pltpu.make_async_copy(
            cache_hbm.at[:, cols(x_lo * KEYS + head * HD, HD)], kv.at[x_lo, own_rows], local_sem.at[0]
        ),
        pltpu.make_async_copy(pos_hbm, istage.at[pl.ds(0, 1)], local_sem.at[1]),
        pltpu.make_async_copy(lim_hbm, istage.at[pl.ds(1, 1)], local_sem.at[2]),
        pltpu.make_async_copy(q_hbm.at[0, :, cols(head * WIDE, WIDE)], qbuf.at[head], local_sem.at[3]),
        pltpu.make_async_copy(prefix_hbm.at[:, head], pbuf, local_sem.at[4]),
        pltpu.make_async_copy(freq_hbm, freq, local_sem.at[5]),
    ]
    for cp in lc:
        cp.start()
    eye[...] = jnp.where(
        lax.broadcasted_iota(jnp.int32, (HD, HD), 0) == lax.broadcasted_iota(jnp.int32, (HD, HD), 1), 1.0, 0.0
    ).astype(jnp.bfloat16)
    for cp in lc[:3]:
        cp.wait()

    pl.semaphore_wait(barrier, 17)

    sent = []
    zc = {}
    for k in (1, 7, 3, 2, 6, 5, 4):
        zc[k] = remote(kv.at[x_lo, own_rows], kv.at[x_lo, own_rows], zs.at[k], zr.at[k], xz_dev(k))
        zc[k].start()
        sent.append(zc[k])
    fc = []

    def forward(k):
        rows = shard_rows(k)
        for n in (2, 3, 1):
            cp = remote(kv.at[x_lo, rows], kv.at[x_lo, rows], fs.at[k, n], fr, xz_dev(8 * n))
            cp.start()
            fc.append(cp)
            sent.append(cp)

    qc = {}

    def send_rows(k):
        a = remote(istage, ibuf.at[head], is_.at[k], ir.at[k], yc_dev(k))
        a.start()
        b = remote(q_hbm.at[0, :, cols((head ^ k) * WIDE, WIDE)], qbuf.at[head], qs.at[k], qr.at[k], yc_dev(k))
        b.start()
        qc[k] = (a, b)
        sent.extend(qc[k])

    forward(0)
    for k in (1, 2, 3, 6, 7, 4, 5):
        send_rows(k)
    for k in (1, 7, 3, 2, 6, 5, 4):
        zc[k].wait_recv()
        forward(k)
    ibuf[head] = istage[...]
    for cp in lc[3:]:
        cp.wait()
    pvt[...] = pbuf[1].T

    def arrive(k):
        for cp in qc[k]:
            cp.wait_recv()

    def prep(i, k):
        s = head ^ k
        t, u = prepare(qbuf[s], ibuf[s, 0:1, :], ibuf[s, 1:2, :], freq[...], eye[...])
        tqs[:, i * WIDE : (i + 1) * WIDE] = t
        sqs[:, i * WIDE : (i + 1) * WIDE] = u

    def ahead():
        p, r, o = student_forward(sqs[...], pbuf[0], pvt[...])
        probs[...] = p
        rounded[...] = r
        outs[...] = o

    def rest(ks):
        target = jnp.concatenate(
            [
                teacher(
                    tqs[:, i * WIDE : (i + 2) * WIDE],
                    jnp.concatenate([ibuf[head ^ ks[i], 1:2, :]] * PER + [ibuf[head ^ ks[i + 1], 1:2, :]] * PER, axis=1),
                    kv[0],
                    vt[...],
                )
                for i in range(0, len(ks), 2)
            ],
            axis=1,
        )
        gk, gv, d, t = student_backward(sqs[...], probs[...], rounded[...], outs[...], target, pbuf[1])
        for i, k in enumerate(ks):
            eout[head ^ k, 0:1, :] = heads_sum(d[:, i * WIDE : (i + 1) * WIDE])
            eout[head ^ k, 1:2, :] = heads_sum(t[:, i * WIDE : (i + 1) * WIDE])
        return gk, gv

    first, second = (0, 1, 2, 3), (6, 7, 4, 5)
    prep(0, 0)
    for i, k in enumerate(first[1:]):
        arrive(k)
        prep(i + 1, k)
    ahead()
    three = qbuf.at[pl.ds(0, 3)]
    remote(three, three, fs.at[0, 1], fr, xz_dev(8)).wait_recv()
    vt[...] = kv[1].T
    gk, gv = rest(first)
    grad[0:PRE] = gk
    grad[PRE:] = gv
    for k in second:
        arrive(k)
    for i, k in enumerate(second):
        prep(i, k)
    ahead()
    gk, gv = rest(second)
    grad[0:PRE] += gk
    grad[PRE:] += gv

    for k in PLANE:
        remote(grad.at[piece_rows(k)], rland.at[k], gs, gr, xz_dev(k)).start()
    for k in range(1, 8):
        cp = remote(eout.at[head ^ k], eland.at[head], es.at[k], er.at[k], yc_dev(k))
        cp.start()
        sent.append(cp)
    eland[head] = eout[head]
    rows8 = grad[piece_rows(0), :]
    all31 = rland.at[pl.ds(1, 31)]
    remote(all31, all31, gs, gr, xz_dev(1)).wait_recv()
    for k in range(1, 32):
        rows8 = rows8 + rland[k]
    own8[...] = rows8
    nsend[0:1] = jnp.sum(rows8 * rows8, axis=0, keepdims=True)
    for k in (4, 5, 2, 3, 6, 7, 1):
        remote(nsend.at[pl.ds(0, 1)], nyc.at[pl.ds(k, 1)], ns.at[0], nr.at[0], yc_dev(k)).start()

    @pl.when(jnp.logical_not(own_perm))
    def _():
        remote(own8, fin, ps.at[0], pr.at[0], perm_dev).start()

    @pl.when(own_perm)
    def _():
        fin[...] = own8[...]

    nyc[0:1] = nsend[0:1]
    seven = nyc.at[pl.ds(1, 7)]
    remote(seven, seven, ns.at[0], nr.at[0], yc_dev(1)).wait_recv()
    nsend[1:2] = jnp.sum(nyc[...], axis=0, keepdims=True)
    for k in PLANE:
        remote(nsend.at[pl.ds(1, 1)], nxz.at[pl.ds(k, 1)], ns.at[1], nr.at[1], xz_dev(k)).start()
    nxz[0:1] = nsend[1:2]
    for k in range(1, 8):
        remote(eout.at[k], eland.at[k], es.at[k], er.at[k], yc_dev(k)).wait_recv()
    esum = eland[0]
    for k in range(1, 8):
        esum = esum + eland[k]
    err_ref[...] = jnp.sqrt(esum[0:1] / FEATURES) / jnp.sqrt(esum[1:2] / FEATURES + norm_eps)
    for cp in sent:
        cp.wait_send()
    remote(all31, all31, gs, gr, xz_dev(1)).wait_send()
    remote(seven, seven, ns.at[0], nr.at[0], yc_dev(1)).wait_send()

    @pl.when(jnp.logical_not(own_perm))
    def _():
        remote(own8, fin, ps.at[0], pr.at[0], perm_dev).wait()

    thirty = nxz.at[pl.ds(1, 31)]
    remote(thirty, thirty, ns.at[1], nr.at[1], xz_dev(1)).wait()
    whole = jnp.sum(nxz[...], axis=0, keepdims=True)
    mean_square = jnp.sum(whole, axis=1, keepdims=True) / (2.0 * KVH * PRE * HD)
    step_ref[...] = fin[...] / jnp.sqrt(mean_square + norm_eps)


def frequencies():
    f = (rope_base ** (-np.arange(HD // 2, dtype=np.float64) / (HD // 2))).astype(np.float32)
    return np.broadcast_to(f[:, None], (HD // 2, ROWS)).copy()


def shards(queries, question_pos, cache_limit, cache, prefix):
    freq = jnp.asarray(frequencies())
    vmem = pl.BlockSpec(memory_space=pltpu.VMEM)
    hbm = pl.BlockSpec(memory_space=pltpu.HBM)
    f32, bf16 = jnp.float32, jnp.bfloat16
    dma = pltpu.SemaphoreType.DMA
    return pl.pallas_call(
        kernel,
        out_shape=(
            jax.ShapeDtypeStruct((8, HD), f32),
            jax.ShapeDtypeStruct((1, ROWS), f32),
        ),
        in_specs=[hbm] * 6,
        out_specs=(vmem, vmem),
        scratch_shapes=[
            pltpu.VMEM((8, ROWS, WIDE), bf16),
            pltpu.VMEM((8, 8, ROWS), jnp.int32),
            pltpu.VMEM((8, ROWS), jnp.int32),
            pltpu.VMEM((HD // 2, ROWS), f32),
            pltpu.VMEM((2, POS, HD), bf16),
            pltpu.VMEM((HD, POS), bf16),
            pltpu.VMEM((2, PRE, HD), bf16),
            pltpu.VMEM((HD, PRE), bf16),
            pltpu.VMEM((HD, HD), bf16),
            pltpu.VMEM((2 * PRE, HD), f32),
            pltpu.VMEM((32, 8, HD), f32),
            pltpu.VMEM((8, HD), f32),
            pltpu.VMEM((8, 8, ROWS), f32),
            pltpu.VMEM((8, 8, ROWS), f32),
            pltpu.VMEM((8, HD), f32),
            pltpu.VMEM((8, HD), f32),
            pltpu.VMEM((32, HD), f32),
            pltpu.VMEM((8, HD), f32),
            pltpu.VMEM((HD, 4 * WIDE), bf16),
            pltpu.VMEM((HD, 4 * WIDE), bf16),
            pltpu.VMEM((PRE, 4 * WIDE), f32),
            pltpu.VMEM((PRE, 4 * WIDE), bf16),
            pltpu.VMEM((HD, 4 * WIDE), f32),
            dma((6,)),
            dma((8,)), dma((8,)), dma((8,)), dma((8,)), dma((8,)), dma((8,)), dma((8, 4)), dma,
            dma((8,)), dma((8,)), dma, dma, dma((1,)), dma((1,)), dma((2,)), dma((2,)),
        ],
        compiler_params=pltpu.CompilerParams(
            collective_id=0, has_side_effects=True, vmem_limit_bytes=60 * 1024 * 1024
        ),
        cost_estimate=pl.CostEstimate(
            flops=3_000_000_000, bytes_accessed=4_000_000, transcendentals=5_000_000
        ),
    )(queries, question_pos, cache_limit, cache, prefix, freq)


def solution(mesh):
    return jax.shard_map(
        shards,
        mesh=mesh,
        in_specs=(P("grp", "blk", None), P("grp", "blk"), P("grp", "blk"), P("blk", None), P()),
        out_specs=(P(("blk", "grp"), None), P("grp", "blk")),
        check_vma=False,
    )
```
